256 devices in a mesh: fsdp: 32 (over z, y), tensor: 8 (over x, core).
Axes of the slice: x: 4, y: 4, z: 8, core: 2. Of those that a mesh axis runs over, the one named last changes fastest.
Arguments:
- mom_square: float32 [2, 8192, 8192], P(None, 'fsdp', 'tensor'), may hold values from -6 to 6
- grad_square: bfloat16 [2, 8192, 8192], P(None, 'fsdp', 'tensor'), may hold values from -6 to 6
- basis_square: float32 [2, 8192, 256], P(None, 'tensor'), may hold values from -0.0625 to 0.0625
- mom_narrow: float32 [2, 8192, 1024], P(None, 'fsdp', 'tensor'), may hold values from -6 to 6
- grad_narrow: bfloat16 [2, 8192, 1024], P(None, 'fsdp', 'tensor'), may hold values from -6 to 6
- basis_narrow: float32 [2, 1024, 256], P(None, 'tensor'), may hold values from -0.1875 to 0.1875
Outputs:
- new_mom_square: float32 [2, 8192, 8192], P(None, 'fsdp', 'tensor')
- update_square: bfloat16 [2, 8192, 8192], P(None, 'fsdp', 'tensor')
- new_basis_square: float32 [2, 8192, 256], P(None, 'tensor')
- new_mom_narrow: float32 [2, 8192, 1024], P(None, 'fsdp', 'tensor')
- update_narrow: bfloat16 [2, 8192, 1024], P(None, 'fsdp', 'tensor')
- new_basis_narrow: float32 [2, 1024, 256], P(None, 'tensor')
The draws below stay inside these ranges and needn't reach their ends.
All inputs are finite; a program needn't handle non-finite values.
Results may differ from the reference program's by a relative error of at most 0.001.
Values sent between devices are 32-bit elements; how exact they have to be, the bound alone decides.
No kernel may reach another device: no remote copies, remote signals or barrier semaphores. Data moves between devices by JAX's collectives and lax.ppermute only.
A program may use at most 64 MiB of HBM per device.

```python
import jax
import jax.numpy as jnp
from jax import lax

D = 8192
KVW = 1024
RANK = 256


def levels(key, extent, shards, smallest, largest):
    def one(axis_at, parts):
        draws = jax.random.uniform(jax.random.fold_in(jax.random.fold_in(key, 6), axis_at), (parts,), jnp.float32, smallest / len(shards), largest / len(shards))
        return jnp.repeat(jnp.exp(draws), extent[axis_at] // parts).reshape((-1,) + (1,) * (len(extent) - axis_at - 1))

    gain = one(*shards[0])
    for cut in shards[1:]:
        gain = gain * one(*cut)
    return gain


def gaussian(own_key, shape, width, most, split=(), held_as=jnp.bfloat16):
    result = width * jax.random.normal(own_key, shape, jnp.float32)
    if split:
        result = result * levels(own_key, shape, split, -0.22, 0.18)
    return jnp.clip(result, -most, most).astype(held_as)


def setup_inputs(seed: int = 0) -> dict:
    splits = jax.random.split(jax.random.key(seed), 7)
    mom_square = gaussian(splits[0], (2, D, D), 1.0, 6.0, ((1, 32), (2, 8)), jnp.float32)
    grad_square = gaussian(splits[1], (2, D, D), 1.0, 6.0, ((1, 32), (2, 8)))
    basis_square = gaussian(splits[2], (2, D, RANK), D ** -0.5, 0.0625, ((1, 8),), jnp.float32)
    mom_narrow = gaussian(splits[3], (2, D, KVW), 1.0, 6.0, ((1, 32), (2, 8)), jnp.float32)
    grad_narrow = gaussian(splits[4], (2, D, KVW), 1.0, 6.0, ((1, 32), (2, 8)))
    basis_narrow = gaussian(splits[5], (2, KVW, RANK), KVW ** -0.5, 0.1875, ((1, 8),), jnp.float32)
    return dict(mom_square=mom_square, grad_square=grad_square, basis_square=basis_square, mom_narrow=mom_narrow, grad_narrow=grad_narrow, basis_narrow=basis_narrow)


HIGH = lax.Precision.HIGHEST

def dion_step(momentum, gradient, basis, columns):
    buffer = momentum + gradient.astype(jnp.float32)
    left = jnp.einsum('kmc,kcr->kmr', buffer, basis, precision=HIGH)
    gram = jnp.einsum('kmr,kms->krs', left, left, precision=HIGH)
    lower = jnp.linalg.cholesky(gram)
    solved = jax.scipy.linalg.solve_triangular(lower, jnp.swapaxes(left, 1, 2), lower=True)
    ortho = jnp.swapaxes(solved, 1, 2)
    right = jnp.einsum('kmc,kmr->kcr', buffer, ortho, precision=HIGH)
    new_momentum = buffer - (1.0 - 0.95) * jnp.einsum('kmr,kcr->kmc', ortho, right, precision=HIGH)
    squares = lax.optimization_barrier(jnp.sum(right * right, axis=1))
    new_basis = right * lax.rsqrt(squares + 1e-06)[:, None, :]
    factor = (D * columns / RANK) ** 0.5
    update = (factor * jnp.einsum('kmr,kcr->kmc', ortho, new_basis, precision=HIGH)).astype(jnp.bfloat16)
    return (new_momentum, update, new_basis)

def reference(mom_square, grad_square, basis_square, mom_narrow, grad_narrow, basis_narrow):
    square_mom, square_update, square_basis = dion_step(mom_square, grad_square, basis_square, D)
    narrow_mom, narrow_update, narrow_basis = dion_step(mom_narrow, grad_narrow, basis_narrow, KVW)
    return (square_mom, square_update, square_basis, narrow_mom, narrow_update, narrow_basis)
```

```python
import functools

import jax
import jax.numpy as jnp
from jax import lax
from jax.experimental import pallas as pl
from jax.experimental.pallas import tpu as pltpu
from jax.sharding import Mesh, PartitionSpec as P

D = 8192
KVW = 1024
RANK = 256

F32 = jnp.float32
BF16 = jnp.bfloat16
AXES = ("zh", "zl", "yh", "yl", "x", "core")
ROWS = ("zh", "zl", "yh", "yl")
COLS = ("x", "core")
FAR = ("zh", "yh")
NN = (((1,), (0,)), ((), ()))
NT = (((1,), (1,)), ((), ()))
TN = (((0,), (0,)), ((), ()))
SQ, NA, GR = 32, 8, 8
CHUNK = 2 * SQ + NA


def split(value):
    high = value.astype(BF16)
    return high, (value - high.astype(F32)).astype(BF16)


def dot3(left, right, dims):
    (lh, ll), (rh, rl) = left, right
    dot = functools.partial(lax.dot_general, dimension_numbers=dims, preferred_element_type=F32)
    return dot(lh, rh) + (dot(lh, rl) + dot(ll, rh))


def call(kernel, outs, operands, scratch=(), name=None):
    vmem = pl.BlockSpec(memory_space=pltpu.VMEM)
    return pl.pallas_call(
        kernel,
        out_shape=[jax.ShapeDtypeStruct(s, d) for s, d in outs],
        in_specs=[pl.BlockSpec(memory_space=pltpu.SMEM)] + [vmem] * (len(operands) - 1),
        out_specs=[vmem] * len(outs),
        scratch_shapes=list(scratch),
        compiler_params=pltpu.CompilerParams(vmem_limit_bytes=50 * 2**20),
        name=name,
    )(*operands)


def project_kernel(place, ms, gs, qs, mn, gn, qn, mine, theirs, left):
    core = place[0]
    for k in range(4):
        m, g, q = (ms, gs, qs) if k < 2 else (mn, gn, qn)
        buffer = split(m[k % 2] + g[k % 2].astype(F32))
        left[k] = dot3(buffer, split(q[k % 2]), NN)
    for x in range(4):
        for k in range(4):
            mine[x, k] = left[k, pl.ds(pl.multiple_of(core * 128 + x * 32, 32), 32), :]
            theirs[x, k] = left[k, pl.ds(pl.multiple_of((1 - core) * 128 + x * 32, 32), 32), :]


def back_kernel(place, ms, gs, mn, gn, own_half, other_half, left, own, to_y, to_z, to_d, w):
    core, x, q = place[0], place[1], place[2]
    for i in range(4):
        for k in range(4):
            left[k, pl.ds(pl.multiple_of(core * 128 + i * 32, 32), 32), :] = own_half[i, k]
            left[k, pl.ds(pl.multiple_of((1 - core) * 128 + i * 32, 32), 32), :] = other_half[i, k]
    for k in range(2):
        buffer = split(ms[k] + gs[k].astype(F32))
        w[:, k * SQ:(k + 1) * SQ, :] = dot3(buffer, split(left[k]), TN).reshape(32, SQ, RANK)
    for k in range(2):
        buffer = split(mn[k] + gn[k].astype(F32))
        w[k * 16:(k + 1) * 16, 2 * SQ:CHUNK, :] = dot3(buffer, split(left[2 + k]), TN).reshape(16, NA, RANK)
    one = split(left[x])
    w[:, CHUNK:, :] = dot3(one, one, TN).reshape(32, GR, RANK)
    for j, out in enumerate((own, to_y, to_z, to_d)):
        out[...] = w[pl.ds((q ^ j) * 8, 8)]


def factor_kernel(place, g0, g1, g2, g3, out, w):
    q = place[2]
    n, nb = RANK, 64
    for j, g in enumerate((g0, g1, g2, g3)):
        w[pl.ds(pl.multiple_of((q ^ j) * 64, 64), 64), :n] = g[...].reshape(64, n)
    row = lax.broadcasted_iota(jnp.int32, (n, n), 0)
    col = lax.broadcasted_iota(jnp.int32, (n, n), 1)
    w[:, n:] = jnp.where(row == col, 1.0, 0.0)
    sub = lax.broadcasted_iota(jnp.int32, (nb, 1), 0)
    for o in range(0, n, nb):
        lo, hi = o // 128 * 128, n + (o + nb + 127) // 128 * 128
        r = w[o:o + nb, lo:hi]
        d = jnp.ones((nb, 1), F32)
        for i in range(nb):
            c = o + i - lo
            pivot = r[i:i + 1, c:c + 1]
            f = jnp.where(sub > i, r[:, c:c + 1] * (1.0 / pivot), 0.0)
            d = jnp.where(sub == i, pivot, d)
            r = r - f * r[i:i + 1, :]
        s = r * lax.rsqrt(d)
        out[o:o + nb, :hi - n] = s[:, n - lo:]
        if hi < 2 * n:
            out[o:o + nb, hi - n:] = jnp.zeros((nb, 2 * n - hi), F32)
        if o + nb < n:
            change = lax.dot_general(
                s[:, :n - lo], s, TN, precision=lax.Precision.HIGHEST, preferred_element_type=F32
            )
            w[o + nb:, lo:hi] = w[o + nb:, lo:hi] - change[o + nb - lo:]


def right_kernel(place, w0, w1, w2, w3, l0, l1, l2, l3, left, ms, gs, mn, gn,
                 right_s, right_n, ortho, squares, mom_s, mom_n, inv):
    x, q = place[1], place[2]
    for d, linv in enumerate((l0, l1, l2, l3)):
        inv[(x - d) & 3] = linv[...]
    for j, w in enumerate((w0, w1, w2, w3)):
        p = q ^ j
        for k in range(2):
            rows = split(w[:, k * SQ:(k + 1) * SQ, :].reshape(8 * SQ, RANK))
            right_s[k, pl.ds(pl.multiple_of(p * 8 * SQ, 8 * SQ), 8 * SQ), :] = dot3(rows, split(inv[k]), NT)
        rows = split(w[:, 2 * SQ:, :].reshape(8 * NA, RANK))
        right_n[p >> 1, pl.ds(pl.multiple_of((p & 1) * 8 * NA, 8 * NA), 8 * NA), :] = dot3(
            rows, split(inv[2 + (p >> 1)]), NT
        )
    squares[...] = jnp.zeros_like(squares)
    for k in range(4):
        m, g, right, mom = (ms, gs, right_s, mom_s) if k < 2 else (mn, gn, right_n, mom_n)
        r = right[k % 2]
        squares[k:k + 1, :] = jnp.sum(r * r, axis=0, keepdims=True)
        o = dot3(split(left[k]), split(inv[k]), NT)
        ortho[k] = o
        low_rank = lax.dot_general(o.astype(BF16), r.astype(BF16), NT, preferred_element_type=F32)
        mom[k % 2] = (m[k % 2] + g[k % 2].astype(F32)) - (1.0 - 0.95) * low_rank


def update_kernel(place, squares, right_s, right_n, ortho, up_s, basis_s, up_n, basis_n):
    scale = lax.rsqrt(jnp.sum(squares[...], axis=0) + 1e-06)
    for k in range(4):
        right, up, basis, columns = (right_s, up_s, basis_s, D) if k < 2 else (right_n, up_n, basis_n, KVW)
        s = scale[k:k + 1, :]
        r = right[k % 2]
        basis[k % 2] = r * s
        o = ortho[k] * (s * (D * columns / RANK) ** 0.5)
        up[k % 2] = dot3(split(o), split(r), NT).astype(BF16)


def partners():
    def pair(i, core, n):
        return i ^ 1 if core == 0 else (((i - 1) ^ 1) + 1) % n

    y_pairs, z_pairs, d_pairs = [], [], []
    for i in range(256):
        z, y, x, core = i // 32, i // 8 % 4, i // 2 % 4, i % 2
        z2, y2 = pair(z, core, 8), pair((y - core) % 4, 0, 4)
        y2 = (y2 + core) % 4
        at = lambda a, b: a * 32 + b * 8 + x * 2 + core
        y_pairs.append((i, at(z, y2)))
        z_pairs.append((i, at(z2, y)))
        d_pairs.append((i, at(z2, y2)))
    return y_pairs, z_pairs, d_pairs


def around_x(value):
    got = {0: value}
    for d in (2, 1, 3):
        got[d] = lax.ppermute(value, "x", [(i, (i + d) % 4) for i in range(4)])
    return [got[d] for d in range(4)]


def swap_core(value):
    return lax.ppermute(value, "core", [(0, 1), (1, 0)])


def local(mom_square, grad_square, basis_square, mom_narrow, grad_narrow, basis_narrow):
    q = lax.axis_index("zl") * 2 + lax.axis_index("yl")
    place = jnp.stack([lax.axis_index("core"), lax.axis_index("x"), q]).astype(jnp.int32)
    in_block = partners()

    mine, theirs = call(
        project_kernel,
        [((4, 4, 32, RANK), F32)] * 2,
        (place, mom_square, grad_square, basis_square, mom_narrow, grad_narrow, basis_narrow),
        [pltpu.VMEM((4, 256, RANK), F32)],
        name="project",
    )
    half = mine + swap_core(theirs)
    part = jnp.sum(lax.all_to_all(half, "x", 0, 0), axis=0)
    own_half = lax.all_to_all(jnp.broadcast_to(part[None], (4,) + part.shape), "x", 0, 0)
    other_half = swap_core(own_half)

    left, own, *send = call(
        back_kernel,
        [((4, 256, RANK), F32)] + [((8, CHUNK + GR, RANK), F32)] * 4,
        (place, mom_square, grad_square, mom_narrow, grad_narrow, own_half, other_half),
        [pltpu.VMEM((32, CHUNK + GR, RANK), F32)],
        name="back",
    )
    for value, pairs in zip(send, in_block):
        own = own + lax.ppermute(value, AXES, pairs)
    part = jnp.sum(lax.all_to_all(own, FAR, 0, 0), axis=0)
    own = lax.all_to_all(jnp.broadcast_to(part[None], (8,) + part.shape), FAR, 0, 0)
    gram = own[:, CHUNK:, :]
    grams = [gram] + [lax.ppermute(gram, AXES, pairs) for pairs in in_block]
    w = own[:, :CHUNK, :]
    ws = [w] + [lax.ppermute(w, AXES, pairs) for pairs in in_block]
    (inverse,) = call(
        factor_kernel,
        [((RANK, RANK), F32)],
        (place, *grams),
        [pltpu.VMEM((RANK, 2 * RANK), F32)],
        name="factor",
    )
    inverses = around_x(inverse)
    right_s, right_n, ortho, squares, new_mom_s, new_mom_n = call(
        right_kernel,
        [((2, 1024, RANK), F32), ((2, 128, RANK), F32), ((4, 256, RANK), F32), ((8, RANK), F32),
         (mom_square.shape, F32), (mom_narrow.shape, F32)],
        (place, *ws, *inverses, left, mom_square, grad_square, mom_narrow, grad_narrow),
        [pltpu.VMEM((4, RANK, RANK), F32)],
        name="right",
    )
    squares = lax.all_to_all(jnp.broadcast_to(squares[None], (8,) + squares.shape), COLS, 0, 0)
    up_s, basis_s, up_n, basis_n = call(
        update_kernel,
        [(mom_square.shape, BF16), (basis_square.shape, F32), (mom_narrow.shape, BF16), (basis_narrow.shape, F32)],
        (place, squares, right_s, right_n, ortho),
        name="update",
    )
    return new_mom_s, up_s, basis_s, new_mom_n, up_n, basis_n


def solution(mesh):
    fine = Mesh(mesh.devices.reshape(4, 2, 2, 2, 4, 2), AXES)
    matrix, factor = P(None, ROWS, COLS), P(None, COLS, None)
    return jax.shard_map(
        local,
        mesh=fine,
        in_specs=(matrix, matrix, factor) * 2,
        out_specs=(matrix, matrix, factor) * 2,
        check_vma=False,
    )
```

```python
import functools

import jax
import jax.numpy as jnp
from jax import lax
from jax.experimental import pallas as pl
from jax.experimental.pallas import tpu as pltpu
from jax.sharding import Mesh, PartitionSpec as P

D = 8192
KVW = 1024
RANK = 256

F32 = jnp.float32
BF16 = jnp.bfloat16
AXES = ("zh", "zl", "yh", "yl", "x", "core")
ROWS = ("zh", "zl", "yh", "yl")
COLS = ("x", "core")
FAR = ("zh", "yh")
NN = (((1,), (0,)), ((), ()))
NT = (((1,), (1,)), ((), ()))
TN = (((0,), (0,)), ((), ()))
SQ, NA, GR = 32, 8, 8
CHUNK = 2 * SQ + NA


def split(value):
    high = value.astype(BF16)
    return high, (value - high.astype(F32)).astype(BF16)


def dot3(left, right, dims):
    (lh, ll), (rh, rl) = left, right
    dot = functools.partial(lax.dot_general, dimension_numbers=dims, preferred_element_type=F32)
    return dot(lh, rh) + (dot(lh, rl) + dot(ll, rh))


def call(kernel, outs, operands, scratch=(), name=None, far_in=(), far_out=()):
    vmem, hbm = pl.BlockSpec(memory_space=pltpu.VMEM), pl.BlockSpec(memory_space=pltpu.HBM)
    return pl.pallas_call(
        kernel,
        out_shape=[jax.ShapeDtypeStruct(s, d) for s, d in outs],
        in_specs=[pl.BlockSpec(memory_space=pltpu.SMEM)]
        + [hbm if i in far_in else vmem for i in range(1, len(operands))],
        out_specs=[hbm if i in far_out else vmem for i in range(len(outs))],
        scratch_shapes=list(scratch),
        compiler_params=pltpu.CompilerParams(vmem_limit_bytes=50 * 2**20),
        name=name,
    )(*[pltpu.with_memory_space_constraint(a, pltpu.HBM) if i in far_in else a for i, a in enumerate(operands)])


def project_kernel(place, ms, gs, qs, mn, gn, qn, mine, theirs, left, m_in, g_in, q_in, mn_in, gn_in, qn_in, sem):
    core = place[0]
    copies = [
        [pltpu.make_async_copy(a.at[k], b.at[k], sem.at[i, k])
         for i, (a, b) in enumerate(((ms, m_in), (gs, g_in), (qs, q_in)))]
        for k in range(2)
    ]
    copies.append([
        pltpu.make_async_copy(a, b, sem.at[3 + i, 0])
        for i, (a, b) in enumerate(((mn, mn_in), (gn, gn_in), (qn, qn_in)))
    ])
    for group in copies:
        for copy in group:
            copy.start()
    for k in range(4):
        if k < 3:
            for copy in copies[k]:
                copy.wait()
        m, g, q = (m_in, g_in, q_in) if k < 2 else (mn_in, gn_in, qn_in)
        buffer = split(m[k % 2] + g[k % 2].astype(F32))
        left[k] = dot3(buffer, split(q[k % 2]), NN)
    for x in range(4):
        for k in range(4):
            mine[x, k] = left[k, pl.ds(pl.multiple_of(core * 128 + x * 32, 32), 32), :]
            theirs[x, k] = left[k, pl.ds(pl.multiple_of((1 - core) * 128 + x * 32, 32), 32), :]


def back_kernel(place, ms, gs, mn, gn, own_half, other_half, left, own, to_y, to_z, to_d, w):
    core, x, q = place[0], place[1], place[2]
    for i in range(4):
        for k in range(4):
            left[k, pl.ds(pl.multiple_of(core * 128 + i * 32, 32), 32), :] = own_half[i, k]
            left[k, pl.ds(pl.multiple_of((1 - core) * 128 + i * 32, 32), 32), :] = other_half[i, k]
    for k in range(2):
        buffer = split(ms[k] + gs[k].astype(F32))
        w[:, k * SQ:(k + 1) * SQ, :] = dot3(buffer, split(left[k]), TN).reshape(32, SQ, RANK)
    for k in range(2):
        buffer = split(mn[k] + gn[k].astype(F32))
        w[k * 16:(k + 1) * 16, 2 * SQ:CHUNK, :] = dot3(buffer, split(left[2 + k]), TN).reshape(16, NA, RANK)
    one = split(left[x])
    w[:, CHUNK:, :] = dot3(one, one, TN).reshape(32, GR, RANK)
    for j, out in enumerate((own, to_y, to_z, to_d)):
        out[...] = w[pl.ds((q ^ j) * 8, 8)]


def factor_kernel(place, g0, g1, g2, g3, out, w):
    q = place[2]
    n, nb, step = RANK, 64, 8
    for j, g in enumerate((g0, g1, g2, g3)):
        w[pl.ds(pl.multiple_of((q ^ j) * 64, 64), 64), :n] = g[...].reshape(64, n)
    row = lax.broadcasted_iota(jnp.int32, (n, n), 0)
    col = lax.broadcasted_iota(jnp.int32, (n, n), 1)
    w[:, n:] = jnp.where(row == col, 1.0, 0.0)
    sub = lax.broadcasted_iota(jnp.int32, (nb, 128), 0)
    for o in range(0, n, nb):
        lo, hi = o // 128 * 128, n + (o + nb + 127) // 128 * 128
        r = [w[o:o + nb, t:t + 128] for t in range(lo, hi, 128)]
        d = jnp.ones((nb, 128), F32)
        for i in range(0, nb, step):
            c = o - lo + i
            cols = [jnp.broadcast_to(r[0][:, c + j:c + j + 1], (nb, 128)) for j in range(step)]
            rows = [[a[i + j:i + j + 1, :] for a in r] for j in range(step)]
            for j in range(step):
                p = i + j
                pivot = cols[j][p:p + 1, :]
                d = jnp.where(sub == p, pivot, d)
                f = jnp.where(sub > p, cols[j] * (1.0 / pivot), 0.0)
                for t in range(j + 1, step):
                    cols[t] = cols[t] - f * cols[t][p:p + 1, :]
                    ft = f[i + t:i + t + 1, :]
                    rows[t] = [a - ft * b for a, b in zip(rows[t], rows[j])]
                r = [a - f * b for a, b in zip(r, rows[j])]
        scale = lax.rsqrt(d)
        s = jnp.concatenate([a * scale for a in r], axis=1)
        half, at = o // 128, o % 128
        out[half, at:at + nb, :] = s[:, n - lo:n - lo + 128]
        if half:
            out[2, at:at + nb, :] = s[:, n - lo + 128:n - lo + 256]
        if o + nb < n:
            change = lax.dot_general(
                s[:, :n - lo], s, TN, precision=lax.Precision.HIGHEST, preferred_element_type=F32
            )
            w[o + nb:, lo:hi] = w[o + nb:, lo:hi] - change[o + nb - lo:]


def fill_inverse(inv, blocks):
    for k in range(4):
        inv[k, :128, :128] = blocks[k, 0]
        inv[k, :128, 128:] = jnp.zeros((128, 128), F32)
        inv[k, 128:, :128] = blocks[k, 1]
        inv[k, 128:, 128:] = blocks[k, 2]


def right_kernel(place, w0, w1, w2, w3, blocks, right_s, right_n, squares, inv):
    q = place[2]
    fill_inverse(inv, blocks)
    for j, w in enumerate((w0, w1, w2, w3)):
        p = q ^ j
        for k in range(2):
            rows = split(w[:, k * SQ:(k + 1) * SQ, :].reshape(8 * SQ, RANK))
            right_s[k, pl.ds(pl.multiple_of(p * 8 * SQ, 8 * SQ), 8 * SQ), :] = dot3(rows, split(inv[k]), NT)
        rows = split(w[:, 2 * SQ:, :].reshape(8 * NA, RANK))
        right_n[p >> 1, pl.ds(pl.multiple_of((p & 1) * 8 * NA, 8 * NA), 8 * NA), :] = dot3(
            rows, split(inv[2 + (p >> 1)]), NT
        )
    squares[...] = jnp.zeros_like(squares)
    for k in range(4):
        r = (right_s if k < 2 else right_n)[k % 2]
        squares[k:k + 1, :] = jnp.sum(r * r, axis=0, keepdims=True)


def momentum_kernel(place, blocks, right_s, right_n, left, ms, gs, mn, gn, ortho, mom_s, mom_n, inv, s_out, n_out, sem):
    fill_inverse(inv, blocks)
    copies = []
    for k in range(4):
        m, g, right, mom, new = (ms, gs, right_s, mom_s, s_out) if k < 2 else (mn, gn, right_n, mom_n, n_out)
        o = dot3(split(left[k]), split(inv[k]), NT)
        ortho[k] = o
        low_rank = lax.dot_general(o.astype(BF16), right[k % 2].astype(BF16), NT, preferred_element_type=F32)
        new[k % 2] = (m[k % 2] + g[k % 2].astype(F32)) - (1.0 - 0.95) * low_rank
        copies.append(pltpu.make_async_copy(new.at[k % 2], mom.at[k % 2], sem.at[k]))
        copies[k].start()
    for copy in copies:
        copy.wait()


def update_kernel(place, q0, q1, q2, q3, right_s, right_n, ortho, up_s, basis_s, up_n, basis_n,
                  us_out, bs_out, un_out, bn_out, sem):
    scale = lax.rsqrt((q0[...] + q1[...]) + (q2[...] + q3[...]) + 1e-06)
    copies = []
    for k in range(4):
        right, up, basis, columns, u_out, b_out = (
            (right_s, up_s, basis_s, D, us_out, bs_out) if k < 2 else (right_n, up_n, basis_n, KVW, un_out, bn_out)
        )
        s = scale[k:k + 1, :]
        r = right[k % 2]
        b_out[k % 2] = r * s
        copies.append(pltpu.make_async_copy(b_out.at[k % 2], basis.at[k % 2], sem.at[0, k]))
        copies[-1].start()
        o = ortho[k] * (s * (D * columns / RANK) ** 0.5)
        u_out[k % 2] = dot3(split(o), split(r), NT).astype(BF16)
        copies.append(pltpu.make_async_copy(u_out.at[k % 2], up.at[k % 2], sem.at[1, k]))
        copies[-1].start()
    for copy in copies:
        copy.wait()


def partners():
    def pair(i, core, n):
        return i ^ 1 if core == 0 else (((i - 1) ^ 1) + 1) % n

    y_pairs, z_pairs, d_pairs = [], [], []
    for i in range(256):
        z, y, x, core = i // 32, i // 8 % 4, i // 2 % 4, i % 2
        z2, y2 = pair(z, core, 8), pair((y - core) % 4, 0, 4)
        y2 = (y2 + core) % 4
        at = lambda a, b: a * 32 + b * 8 + x * 2 + core
        y_pairs.append((i, at(z, y2)))
        z_pairs.append((i, at(z2, y)))
        d_pairs.append((i, at(z2, y2)))
    return y_pairs, z_pairs, d_pairs


def around_x(value):
    got = {0: value}
    for d in (2, 1, 3):
        got[d] = lax.ppermute(value, "x", [(i, (i + d) % 4) for i in range(4)])
    return [got[d] for d in range(4)]


def swap_core(value):
    return lax.ppermute(value, "core", [(0, 1), (1, 0)])


def local(mom_square, grad_square, basis_square, mom_narrow, grad_narrow, basis_narrow):
    q = lax.axis_index("zl") * 2 + lax.axis_index("yl")
    place = jnp.stack([lax.axis_index("core"), lax.axis_index("x"), q]).astype(jnp.int32)
    in_block = partners()

    mine, theirs = call(
        project_kernel,
        [((4, 4, 32, RANK), F32)] * 2,
        (place, mom_square, grad_square, basis_square, mom_narrow, grad_narrow, basis_narrow),
        [pltpu.VMEM((4, 256, RANK), F32)]
        + [pltpu.VMEM(a.shape, a.dtype)
           for a in (mom_square, grad_square, basis_square, mom_narrow, grad_narrow, basis_narrow)]
        + [pltpu.SemaphoreType.DMA((6, 2))],
        name="project",
        far_in=range(1, 7),
    )
    half = mine + swap_core(theirs)
    part = jnp.sum(lax.all_to_all(half, "x", 0, 0), axis=0)
    own_half = lax.all_to_all(jnp.broadcast_to(part[None], (4,) + part.shape), "x", 0, 0)
    other_half = swap_core(own_half)

    left, own, *send = call(
        back_kernel,
        [((4, 256, RANK), F32)] + [((8, CHUNK + GR, RANK), F32)] * 4,
        (place, mom_square, grad_square, mom_narrow, grad_narrow, own_half, other_half),
        [pltpu.VMEM((32, CHUNK + GR, RANK), F32)],
        name="back",
    )
    for value, pairs in zip(send, in_block):
        own = own + lax.ppermute(value, AXES, pairs)
    part = jnp.sum(lax.all_to_all(own, FAR, 0, 0), axis=0)
    own = lax.all_to_all(jnp.broadcast_to(part[None], (8,) + part.shape), FAR, 0, 0)
    gram = own[:, CHUNK:, :]
    grams = [gram] + [lax.ppermute(gram, AXES, pairs) for pairs in in_block]
    w = own[:, :CHUNK, :]
    ws = [w] + [lax.ppermute(w, AXES, pairs) for pairs in in_block]
    (blocks,) = call(
        factor_kernel,
        [((3, 128, 128), F32)],
        (place, *grams),
        [pltpu.VMEM((RANK, 2 * RANK), F32)],
        name="factor",
    )
    blocks = lax.all_to_all(jnp.broadcast_to(blocks[None], (4,) + blocks.shape), "x", 0, 0)
    inverse = pltpu.VMEM((4, RANK, RANK), F32)
    right_s, right_n, squares = call(
        right_kernel,
        [((2, 1024, RANK), F32), ((2, 128, RANK), F32), ((8, RANK), F32)],
        (place, *ws, blocks),
        [inverse],
        name="right",
    )
    squares, left = lax.optimization_barrier((squares + swap_core(squares), left))
    four_squares = around_x(squares)
    ortho, new_mom_s, new_mom_n = call(
        momentum_kernel,
        [((4, 256, RANK), F32), (mom_square.shape, F32), (mom_narrow.shape, F32)],
        (place, blocks, right_s, right_n, left, mom_square, grad_square, mom_narrow, grad_narrow),
        [inverse, pltpu.VMEM(mom_square.shape, F32), pltpu.VMEM(mom_narrow.shape, F32), pltpu.SemaphoreType.DMA((4,))],
        name="momentum",
        far_out=(1, 2),
    )
    outs = [(mom_square.shape, BF16), (basis_square.shape, F32), (mom_narrow.shape, BF16), (basis_narrow.shape, F32)]
    up_s, basis_s, up_n, basis_n = call(
        update_kernel,
        outs,
        (place, *four_squares, right_s, right_n, ortho),
        [pltpu.VMEM(s, d) for s, d in outs] + [pltpu.SemaphoreType.DMA((2, 4))],
        name="update",
        far_out=range(4),
    )
    return new_mom_s, up_s, basis_s, new_mom_n, up_n, basis_n


def solution(mesh):
    fine = Mesh(mesh.devices.reshape(4, 2, 2, 2, 4, 2), AXES)
    matrix, factor = P(None, ROWS, COLS), P(None, COLS, None)
    return jax.shard_map(
        local,
        mesh=fine,
        in_specs=(matrix, matrix, factor) * 2,
        out_specs=(matrix, matrix, factor) * 2,
        check_vma=False,
    )
```

```python
import functools

import jax
import jax.numpy as jnp
from jax import lax
from jax.experimental import pallas as pl
from jax.experimental.pallas import tpu as pltpu
from jax.sharding import Mesh, PartitionSpec as P

D = 8192
KVW = 1024
RANK = 256

F32 = jnp.float32
BF16 = jnp.bfloat16
AXES = ("zh", "zl", "yh", "yl", "x", "core")
ROWS = ("zh", "zl", "yh", "yl")
COLS = ("x", "core")
NN = (((1,), (0,)), ((), ()))
NT = (((1,), (1,)), ((), ()))
TN = (((0,), (0,)), ((), ()))
SQ, NA = 32, 8
CHUNK = 2 * SQ + NA


def split(value):
    high = value.astype(BF16)
    return high, (value - high.astype(F32)).astype(BF16)


def dot3(left, right, dims):
    (lh, ll), (rh, rl) = left, right
    dot = functools.partial(lax.dot_general, dimension_numbers=dims, preferred_element_type=F32)
    return dot(lh, rh) + (dot(lh, rl) + dot(ll, rh))


def call(kernel, outs, operands, scratch=(), name=None, far_in=(), far_out=()):
    vmem, hbm = pl.BlockSpec(memory_space=pltpu.VMEM), pl.BlockSpec(memory_space=pltpu.HBM)
    return pl.pallas_call(
        kernel,
        out_shape=[jax.ShapeDtypeStruct(s, d) for s, d in outs],
        in_specs=[pl.BlockSpec(memory_space=pltpu.SMEM)]
        + [hbm if i in far_in else vmem for i in range(1, len(operands))],
        out_specs=[hbm if i in far_out else vmem for i in range(len(outs))],
        scratch_shapes=list(scratch),
        compiler_params=pltpu.CompilerParams(vmem_limit_bytes=28 * 2**20),
        name=name,
    )(*[pltpu.with_memory_space_constraint(a, pltpu.HBM) if i in far_in else a for i, a in enumerate(operands)])


def project_kernel(place, ms, gs, qs, mn, gn, qn, mine, theirs, left, m_in, g_in, q_in, mn_in, gn_in, qn_in, sem):
    core = place[0]
    copies = [
        [pltpu.make_async_copy(a.at[k], b.at[k], sem.at[i, k])
         for i, (a, b) in enumerate(((ms, m_in), (gs, g_in), (qs, q_in)))]
        for k in range(2)
    ]
    copies.append([
        pltpu.make_async_copy(a, b, sem.at[3 + i, 0])
        for i, (a, b) in enumerate(((mn, mn_in), (gn, gn_in), (qn, qn_in)))
    ])
    for group in copies:
        for copy in group:
            copy.start()
    for k in range(4):
        if k < 3:
            for copy in copies[k]:
                copy.wait()
        m, g, q = (m_in, g_in, q_in) if k < 2 else (mn_in, gn_in, qn_in)
        buffer = split(m[k % 2] + g[k % 2].astype(F32))
        left[k] = dot3(buffer, split(q[k % 2]), NN)
    for x in range(4):
        for k in range(4):
            mine[x, k] = left[k, pl.ds(pl.multiple_of(core * 128 + x * 32, 32), 32), :]
            theirs[x, k] = left[k, pl.ds(pl.multiple_of((1 - core) * 128 + x * 32, 32), 32), :]


def back_kernel(place, ms, gs, mn, gn, own_half, other_half, left, gram, own, to_y, to_z, to_d, w):
    core, x, q = place[0], place[1], place[2]
    for i in range(4):
        for k in range(4):
            left[k, pl.ds(pl.multiple_of(core * 128 + i * 32, 32), 32), :] = own_half[i, k]
            left[k, pl.ds(pl.multiple_of((1 - core) * 128 + i * 32, 32), 32), :] = other_half[i, k]
    for k in range(2):
        buffer = split(ms[k] + gs[k].astype(F32))
        w[:, k * SQ:(k + 1) * SQ, :] = dot3(buffer, split(left[k]), TN).reshape(32, SQ, RANK)
    for k in range(2):
        buffer = split(mn[k] + gn[k].astype(F32))
        w[k * 16:(k + 1) * 16, 2 * SQ:, :] = dot3(buffer, split(left[2 + k]), TN).reshape(16, NA, RANK)
    one = split(left[x])
    gram[...] = dot3(one, one, TN).reshape(32, 8, RANK)
    for j, out in enumerate((own, to_y, to_z, to_d)):
        out[...] = w[pl.ds((q ^ j) * 8, 8)]


def factor_kernel(place, gram, out, w):
    n, nb, step = RANK, 64, 8
    w[:, :n] = gram[...]
    row = lax.broadcasted_iota(jnp.int32, (n, n), 0)
    col = lax.broadcasted_iota(jnp.int32, (n, n), 1)
    w[:, n:] = jnp.where(row == col, 1.0, 0.0)
    sub = lax.broadcasted_iota(jnp.int32, (nb, 128), 0)
    for o in range(0, n, nb):
        lo, hi = o // 128 * 128, n + (o + nb + 127) // 128 * 128
        r = [w[o:o + nb, t:t + 128] for t in range(lo, hi, 128)]
        d = jnp.ones((nb, 128), F32)
        for i in range(0, nb, step):
            c = o - lo + i
            cols = [jnp.broadcast_to(r[0][:, c + j:c + j + 1], (nb, 128)) for j in range(step)]
            rows = [[a[i + j:i + j + 1, :] for a in r] for j in range(step)]
            for j in range(step):
                p = i + j
                pivot = cols[j][p:p + 1, :]
                d = jnp.where(sub == p, pivot, d)
                f = jnp.where(sub > p, cols[j] * (1.0 / pivot), 0.0)
                for t in range(j + 1, step):
                    cols[t] = cols[t] - f * cols[t][p:p + 1, :]
                    ft = f[i + t:i + t + 1, :]
                    rows[t] = [a - ft * b for a, b in zip(rows[t], rows[j])]
                r = [a - f * b for a, b in zip(r, rows[j])]
        scale = lax.rsqrt(d)
        s = jnp.concatenate([a * scale for a in r], axis=1)
        half, at = o // 128, o % 128
        out[half, at:at + nb, :] = s[:, n - lo:n - lo + 128]
        if half:
            out[2, at:at + nb, :] = s[:, n - lo + 128:n - lo + 256]
        if o + nb < n:
            change = lax.dot_general(
                s[:, :n - lo], s, TN, precision=lax.Precision.HIGHEST, preferred_element_type=F32
            )
            w[o + nb:, lo:hi] = w[o + nb:, lo:hi] - change[o + nb - lo:]


def fill_inverse(inv, place, around):
    for d, blocks in enumerate(around):
        k = (place[1] - d) & 3
        inv[k, :128, :128] = blocks[0]
        inv[k, :128, 128:] = jnp.zeros((128, 128), F32)
        inv[k, 128:, :128] = blocks[1]
        inv[k, 128:, 128:] = blocks[2]


def right_kernel(place, w0, w1, w2, w3, l0, l1, l2, l3, right, squares, inv, w):
    q, b, yh = place[2], place[3], place[4]
    fill_inverse(inv, place, (l0, l1, l2, l3))
    for j, pair in enumerate((w0, w1, w2, w3)):
        for a in range(2):
            w[a * 4 + (b ^ (j >> 1)) * 2 + (yh ^ (j & 1))] = pair[a]
    row = lax.broadcasted_iota(jnp.int32, (8, RANK), 0)
    total = jnp.zeros((8, RANK), F32)
    for k in range(3):
        at, size, matrix = (k * SQ, SQ, k) if k < 2 else (2 * SQ, NA, 2 + (q >> 1))
        r = dot3(split(w[:, at:at + size, :].reshape(8 * size, RANK)), split(inv[matrix]), NT)
        right[:, at:at + size, :] = r.reshape(8, size, RANK)
        total = total + jnp.where(row == matrix, jnp.sum(r * r, axis=0, keepdims=True), 0.0)
    squares[...] = total


def ortho_kernel(place, l0, l1, l2, l3, left, ortho, inv):
    fill_inverse(inv, place, (l0, l1, l2, l3))
    for k in range(4):
        ortho[k] = dot3(split(left[k]), split(inv[k]), NT)


def finish_kernel(place, r0, r1, r2, r3, squares, ortho, ms, gs, mn, gn, mom_s, up_s, basis_s, mom_n, up_n, basis_n,
                  ms_out, us_out, bs_out, mn_out, un_out, bn_out, narrow, sem):
    q = place[2]
    scale = lax.rsqrt(squares[...] + 1e-06)
    copies = []

    def one(k, r, at):
        m, g, mom, up, basis, columns = (
            (ms, gs, ms_out, us_out, bs_out, D) if k < 2 else (mn, gn, mn_out, un_out, bn_out, KVW)
        )
        s = scale[k:k + 1, :]
        o = ortho[k]
        high, low = split(r)
        basis[k % 2, at, :] = r * s
        low_rank = lax.dot_general(o.astype(BF16), high, NT, preferred_element_type=F32)
        mom[k % 2, :, at] = (m[k % 2, :, at] + g[k % 2, :, at].astype(F32)) - (1.0 - 0.95) * low_rank
        scaled = split(o * (s * (D * columns / RANK) ** 0.5))
        up[k % 2, :, at] = dot3(scaled, (high, low), NT).astype(BF16)

    def send(k):
        pairs = ((ms_out, mom_s), (us_out, up_s), (bs_out, basis_s)) if k < 2 else (
            (mn_out, mom_n), (un_out, up_n), (bn_out, basis_n))
        for i, (source, target) in enumerate(pairs):
            copies.append(pltpu.make_async_copy(source.at[k % 2], target.at[k % 2], sem.at[i, k]))
            copies[-1].start()

    pieces = (r0, r1, r2, r3)
    for k in range(2):
        for j, piece in enumerate(pieces):
            at = pl.ds(pl.multiple_of((q ^ j) * 256, 256), 256)
            one(k, piece[:, k * SQ:(k + 1) * SQ, :].reshape(8 * SQ, RANK), at)
        send(k)
    for j, piece in enumerate(pieces):
        narrow[pl.ds(pl.multiple_of((q ^ j) * 64, 64), 64), :] = piece[:, 2 * SQ:, :].reshape(8 * NA, RANK)
    for k in range(2, 4):
        one(k, narrow[(k - 2) * 128:(k - 1) * 128, :], slice(0, 128))
        send(k)
    for copy in copies:
        copy.wait()


def partners():
    def pair(i, core, n):
        return ((i - core) % n ^ 1) + core

    def perm(move):
        at = [(i // 32, i // 8 % 4, i // 2 % 4, i % 2) for i in range(256)]
        out = []
        for i, (z, y, x, core) in enumerate(at):
            z, y = move(z, y, core)
            out.append((i, z % 8 * 32 + y % 4 * 8 + x * 2 + core))
        return out

    near_z = lambda z, core: pair(z, core, 8)
    near_y = lambda y, core: pair(y, core, 4)
    far_z = lambda z, core: pair(z // 2, core, 4) * 2 + z % 2
    near = [
        perm(lambda z, y, c: (z, near_y(y, c))),
        perm(lambda z, y, c: (near_z(z, c), y)),
        perm(lambda z, y, c: (near_z(z, c), near_y(y, c))),
    ]
    far = [
        perm(lambda z, y, c: (z, y + 2)),
        perm(lambda z, y, c: (far_z(z, c), y)),
        perm(lambda z, y, c: (far_z(z, c), y + 2)),
    ]
    return near, far, perm(lambda z, y, c: (z + 4, y))


def around_x(value):
    got = {0: value}
    for d in (2, 1, 3):
        got[d] = lax.ppermute(value, "x", [(i, (i + d) % 4) for i in range(4)])
    return [got[d] for d in range(4)]


def swap_core(value):
    return lax.ppermute(value, "core", [(0, 1), (1, 0)])


def local(mom_square, grad_square, basis_square, mom_narrow, grad_narrow, basis_narrow):
    zh, yh = lax.axis_index("zh"), lax.axis_index("yh")
    a, b = zh // 2, zh % 2
    q = lax.axis_index("zl") * 2 + lax.axis_index("yl")
    place = jnp.stack([lax.axis_index("core"), lax.axis_index("x"), q, b, yh]).astype(jnp.int32)
    near, far, across = partners()
    send = lambda value, pairs: lax.ppermute(value, AXES, pairs)
    spread = lambda value, axes, n: lax.all_to_all(jnp.broadcast_to(value[None], (n,) + value.shape), axes, 0, 0)
    inputs = (mom_square, grad_square, basis_square, mom_narrow, grad_narrow, basis_narrow)

    mine, theirs = call(
        project_kernel,
        [((4, 4, 32, RANK), F32)] * 2,
        (place,) + inputs,
        [pltpu.VMEM((4, 256, RANK), F32)]
        + [pltpu.VMEM(v.shape, v.dtype) for v in inputs]
        + [pltpu.SemaphoreType.DMA((6, 2))],
        name="project",
        far_in=range(1, 7),
    )
    half = mine + swap_core(theirs)
    part = jnp.sum(lax.all_to_all(half, "x", 0, 0), axis=0)
    own_half = spread(part, "x", 4)
    other_half = swap_core(own_half)

    left, gram, own, *others = call(
        back_kernel,
        [((4, 256, RANK), F32), ((32, 8, RANK), F32)] + [((8, CHUNK, RANK), F32)] * 4,
        (place, mom_square, grad_square, mom_narrow, grad_narrow, own_half, other_half),
        [pltpu.VMEM((32, CHUNK, RANK), F32)],
        name="back",
    )
    got = [send(value, pairs) for value, pairs in zip(others, near)]
    gram, got = lax.optimization_barrier((jnp.sum(lax.all_to_all(gram, ROWS, 0, 0), axis=0), got))
    own = (own + got[0] + got[1] + got[2]).reshape(2, 2, 2, CHUNK, RANK)
    take = lambda i, j: lax.dynamic_slice(own, (0, i, j, 0, 0), (2, 1, 1, CHUNK, RANK)).reshape(2, CHUNK, RANK)
    got = [send(value, pairs) for value, pairs in zip((take(b, 1 - yh), take(1 - b, yh), take(1 - b, 1 - yh)), far)]
    gram, got = lax.optimization_barrier((spread(gram, ROWS, 32), got))
    own = take(b, yh) + got[0] + got[1] + got[2]
    got = send(lax.dynamic_index_in_dim(own, 1 - a, 0, keepdims=False), across)
    (blocks,) = call(
        factor_kernel,
        [((3, 128, 128), F32)],
        (place, gram.reshape(RANK, RANK)),
        [pltpu.VMEM((RANK, 2 * RANK), F32)],
        name="factor",
    )
    blocks, got = lax.optimization_barrier((blocks, got))
    own = lax.dynamic_index_in_dim(own, a, 0, keepdims=False) + got
    got = send(own, across)
    pair = jnp.where(a == 0, jnp.stack([own, got]), jnp.stack([got, own]))
    pairs = [pair] + [send(pair, p) for p in far]
    around = around_x(blocks)
    inverse = pltpu.VMEM((4, RANK, RANK), F32)
    right, squares = call(
        right_kernel,
        [((8, CHUNK, RANK), F32), ((8, RANK), F32)],
        (place, *pairs, *around),
        [inverse, pltpu.VMEM((8, CHUNK, RANK), F32)],
        name="right",
    )
    rights = [right] + [send(right, p) for p in near]
    squares = jnp.sum(spread(squares, ("zl", "yl", "x", "core"), 32), axis=0)
    (ortho,) = call(ortho_kernel, [((4, 256, RANK), F32)], (place, *around, left), [inverse], name="ortho")
    outs = [(v.shape, d) for v, d in zip(
        (mom_square, mom_square, basis_square, mom_narrow, mom_narrow, basis_narrow), (F32, BF16, F32) * 2)]
    return tuple(call(
        finish_kernel,
        outs,
        (place, *rights, squares, ortho, mom_square, grad_square, mom_narrow, grad_narrow),
        [pltpu.VMEM(*o) for o in outs] + [pltpu.VMEM((256, RANK), F32), pltpu.SemaphoreType.DMA((3, 4))],
        name="finish",
        far_out=range(6),
    ))


def solution(mesh):
    fine = Mesh(mesh.devices.reshape(4, 2, 2, 2, 4, 2), AXES)
    matrix, factor = P(None, ROWS, COLS), P(None, COLS, None)
    return jax.shard_map(
        local,
        mesh=fine,
        in_specs=(matrix, matrix, factor) * 2,
        out_specs=(matrix, matrix, factor) * 2,
        check_vma=False,
    )
```

```python
import functools

import jax
import jax.numpy as jnp
from jax import lax
from jax.experimental import pallas as pl
from jax.experimental.pallas import tpu as pltpu
from jax.sharding import Mesh, PartitionSpec as P

D = 8192
KVW = 1024
RANK = 256

F32 = jnp.float32
BF16 = jnp.bfloat16
AXES = ("zh", "zl", "yh", "yl", "x", "core")
ROWS = ("zh", "zl", "yh", "yl")
COLS = ("x", "core")
NN = (((1,), (0,)), ((), ()))
NT = (((1,), (1,)), ((), ()))
TN = (((0,), (0,)), ((), ()))
SQ, NA = 32, 8
CHUNK = 2 * SQ + NA


def split(value):
    high = value.astype(BF16)
    return high, (value - high.astype(F32)).astype(BF16)


def dot3(left, right, dims):
    (lh, ll), (rh, rl) = left, right
    dot = functools.partial(lax.dot_general, dimension_numbers=dims, preferred_element_type=F32)
    return dot(lh, rh) + (dot(lh, rl) + dot(ll, rh))


def call(kernel, outs, operands, scratch=(), name=None, far_in=(), far_out=()):
    vmem, hbm = pl.BlockSpec(memory_space=pltpu.VMEM), pl.BlockSpec(memory_space=pltpu.HBM)
    return pl.pallas_call(
        kernel,
        out_shape=[jax.ShapeDtypeStruct(s, d) for s, d in outs],
        in_specs=[pl.BlockSpec(memory_space=pltpu.SMEM)]
        + [hbm if i in far_in else vmem for i in range(1, len(operands))],
        out_specs=[hbm if i in far_out else vmem for i in range(len(outs))],
        scratch_shapes=list(scratch),
        compiler_params=pltpu.CompilerParams(vmem_limit_bytes=20 * 2**20),
        name=name,
    )(*[pltpu.with_memory_space_constraint(a, pltpu.HBM) if i in far_in else a for i, a in enumerate(operands)])


def project_kernel(place, ms, gs, qs, mn, gn, qn, mine, theirs, left, m_in, g_in, q_in, mn_in, gn_in, qn_in, sem):
    core = place[0]
    copies = [
        [pltpu.make_async_copy(a.at[k], b.at[k], sem.at[i, k])
         for i, (a, b) in enumerate(((ms, m_in), (gs, g_in), (qs, q_in)))]
        for k in range(2)
    ]
    copies.append([
        pltpu.make_async_copy(a, b, sem.at[3 + i, 0])
        for i, (a, b) in enumerate(((mn, mn_in), (gn, gn_in), (qn, qn_in)))
    ])
    for group in copies:
        for copy in group:
            copy.start()
    for k in range(4):
        if k < 3:
            for copy in copies[k]:
                copy.wait()
        m, g, q = (m_in, g_in, q_in) if k < 2 else (mn_in, gn_in, qn_in)
        buffer = split(m[k % 2] + g[k % 2].astype(F32))
        left[k] = dot3(buffer, split(q[k % 2]), NN)
    for x in range(4):
        for k in range(4):
            mine[x, k] = left[k, pl.ds(pl.multiple_of(core * 128 + x * 32, 32), 32), :]
            theirs[x, k] = left[k, pl.ds(pl.multiple_of((1 - core) * 128 + x * 32, 32), 32), :]


def fetch(sources, targets, sem):
    copies = [pltpu.make_async_copy(a, b, sem.at[i]) for i, (a, b) in enumerate(zip(sources, targets))]
    for copy in copies:
        copy.start()
    return copies


def back_kernel(place, ms, gs, mn, gn, own_half, other_half, left, own, to_y, to_z, to_d,
                w, gram, ms_in, gs_in, mn_in, gn_in, sem):
    copies = fetch((ms, gs, mn, gn), (ms_in, gs_in, mn_in, gn_in), sem)
    core, x, q = place[0], place[1], place[2]
    for i in range(4):
        for k in range(4):
            left[k, pl.ds(pl.multiple_of(core * 128 + i * 32, 32), 32), :] = own_half[i, k]
            left[k, pl.ds(pl.multiple_of((1 - core) * 128 + i * 32, 32), 32), :] = other_half[i, k]
    half = left[x, :, pl.ds(pl.multiple_of(core * 128, 128), 128)]
    gram[...] = dot3(split(half), split(left[x]), TN)
    for copy in copies:
        copy.wait()
    for k in range(2):
        buffer = split(ms_in[k] + gs_in[k].astype(F32))
        w[:, k * SQ:(k + 1) * SQ, :] = dot3(buffer, split(left[k]), TN).reshape(32, SQ, RANK)
    for k in range(2):
        buffer = split(mn_in[k] + gn_in[k].astype(F32))
        w[k * 16:(k + 1) * 16, 2 * SQ:, :] = dot3(buffer, split(left[2 + k]), TN).reshape(16, NA, RANK)
    for j, out in enumerate((own, to_y, to_z, to_d)):
        out[:8 * CHUNK] = w[pl.ds((q ^ j) * 8, 8)].reshape(8 * CHUNK, RANK)
        out[8 * CHUNK:] = gram[pl.ds(pl.multiple_of((q ^ j) * 32, 32), 32), :]


def meet_kernel(place, own, r0, r1, r2, mine, to_y, to_z, to_d):
    b, yh = place[3], place[4]
    meet = lambda at: (own[at, :] + r0[at, :]) + (r1[at, :] + r2[at, :])
    gram = meet(slice(8 * CHUNK, None))
    for j, out in enumerate((mine, to_y, to_z, to_d)):
        for a in range(2):
            i = a * 4 + (b ^ (j >> 1)) * 2 + (yh ^ (j & 1))
            out[a * CHUNK:(a + 1) * CHUNK] = meet(pl.ds(pl.multiple_of(i * CHUNK, CHUNK), CHUNK))
        out[2 * CHUNK:] = gram


def factor_kernel(place, g0, g1, g2, g3, out, w):
    n, nb, step = RANK, 64, 8
    for j, g in enumerate((g0, g1, g2, g3)):
        for half in range(2):
            w[pl.ds(pl.multiple_of(half * 128 + (place[2] ^ j) * 32, 32), 32), :n] = g[half]
    row = lax.broadcasted_iota(jnp.int32, (n, n), 0)
    col = lax.broadcasted_iota(jnp.int32, (n, n), 1)
    w[:, n:] = jnp.where(row == col, 1.0, 0.0)
    sub = lax.broadcasted_iota(jnp.int32, (nb, 128), 0)
    for o in range(0, n, nb):
        lo, hi = o // 128 * 128, n + (o + nb + 127) // 128 * 128
        r = [w[o:o + nb, t:t + 128] for t in range(lo, hi, 128)]
        d = jnp.ones((nb, 128), F32)
        for i in range(0, nb, step):
            c = o - lo + i
            cols = [jnp.broadcast_to(r[0][:, c + j:c + j + 1], (nb, 128)) for j in range(step)]
            rows = [[a[i + j:i + j + 1, :] for a in r] for j in range(step)]
            for j in range(step):
                p = i + j
                pivot = cols[j][p:p + 1, :]
                d = jnp.where(sub == p, pivot, d)
                f = jnp.where(sub > p, cols[j] * (1.0 / pivot), 0.0)
                for t in range(j + 1, step):
                    cols[t] = cols[t] - f * cols[t][p:p + 1, :]
                    ft = f[i + t:i + t + 1, :]
                    rows[t] = [a - ft * b for a, b in zip(rows[t], rows[j])]
                r = [a - f * b for a, b in zip(r, rows[j])]
        scale = lax.rsqrt(d)
        s = jnp.concatenate([a * scale for a in r], axis=1)
        half, at = o // 128, o % 128
        out[half, at:at + nb, :] = s[:, n - lo:n - lo + 128]
        if half:
            out[2, at:at + nb, :] = s[:, n - lo + 128:n - lo + 256]
        if o + nb < n:
            change = lax.dot_general(
                s[:, :n - lo], s, TN, precision=lax.Precision.HIGHEST, preferred_element_type=F32
            )
            w[o + nb:, lo:hi] = w[o + nb:, lo:hi] - change[o + nb - lo:]


def fill_inverse(inv, place, around):
    for d, blocks in enumerate(around):
        k = (place[1] - d) & 3
        inv[k, :128, :128] = blocks[0]
        inv[k, :128, 128:] = jnp.zeros((128, 128), F32)
        inv[k, 128:, :128] = blocks[1]
        inv[k, 128:, 128:] = blocks[2]


def arrange_kernel(place, w0, w1, w2, w3, out):
    for j, pair in enumerate((w0, w1, w2, w3)):
        for a in range(2):
            out[a * 4 + (place[3] ^ (j >> 1)) * 2 + (place[4] ^ (j & 1))] = pair[a]


def right_kernel(place, w0, w1, w2, w3, l0, l1, l2, l3, right_s, right_n, squares, inv):
    q = place[2]
    fill_inverse(inv, place, (l0, l1, l2, l3))
    for j, w in enumerate((w0, w1, w2, w3)):
        p = q ^ j
        for k in range(2):
            rows = split(w[:, k * SQ:(k + 1) * SQ, :].reshape(8 * SQ, RANK))
            right_s[k, pl.ds(pl.multiple_of(p * 8 * SQ, 8 * SQ), 8 * SQ), :] = dot3(rows, split(inv[k]), NT)
        rows = split(w[:, 2 * SQ:, :].reshape(8 * NA, RANK))
        right_n[p >> 1, pl.ds(pl.multiple_of((p & 1) * 8 * NA, 8 * NA), 8 * NA), :] = dot3(
            rows, split(inv[2 + (p >> 1)]), NT
        )
    squares[...] = jnp.zeros_like(squares)
    for k in range(4):
        r = (right_s if k < 2 else right_n)[k % 2]
        squares[k:k + 1, :] = jnp.sum(r * r, axis=0, keepdims=True)


def momentum_kernel(place, l0, l1, l2, l3, right_s, right_n, left, ms, gs, mn, gn, ortho, mom_s, mom_n, inv, s_out, n_out, sem):
    fill_inverse(inv, place, (l0, l1, l2, l3))
    copies = []
    for k in range(4):
        m, g, right, mom, new = (ms, gs, right_s, mom_s, s_out) if k < 2 else (mn, gn, right_n, mom_n, n_out)
        o = dot3(split(left[k]), split(inv[k]), NT)
        ortho[k] = o
        low_rank = lax.dot_general(o.astype(BF16), right[k % 2].astype(BF16), NT, preferred_element_type=F32)
        new[k % 2] = (m[k % 2] + g[k % 2].astype(F32)) - (1.0 - 0.95) * low_rank
        copies.append(pltpu.make_async_copy(new.at[k % 2], mom.at[k % 2], sem.at[k]))
        copies[k].start()
    for copy in copies:
        copy.wait()


def update_kernel(place, q0, q1, q2, q3, right_s, right_n, ortho, up_s, basis_s, up_n, basis_n,
                  us_out, bs_out, un_out, bn_out, sem):
    scale = lax.rsqrt((q0[...] + q1[...]) + (q2[...] + q3[...]) + 1e-06)
    copies = []
    for k in range(4):
        right, up, basis, columns, u_out, b_out = (
            (right_s, up_s, basis_s, D, us_out, bs_out) if k < 2 else (right_n, up_n, basis_n, KVW, un_out, bn_out)
        )
        s = scale[k:k + 1, :]
        r = right[k % 2]
        b_out[k % 2] = r * s
        copies.append(pltpu.make_async_copy(b_out.at[k % 2], basis.at[k % 2], sem.at[0, k]))
        copies[-1].start()
        o = ortho[k] * (s * (D * columns / RANK) ** 0.5)
        u_out[k % 2] = dot3(split(o), split(r), NT).astype(BF16)
        copies.append(pltpu.make_async_copy(u_out.at[k % 2], up.at[k % 2], sem.at[1, k]))
        copies[-1].start()
    for copy in copies:
        copy.wait()


def partners():
    def pair(i, core, n):
        return ((i - core) % n ^ 1) + core

    def perm(move):
        at = [(i // 32, i // 8 % 4, i // 2 % 4, i % 2) for i in range(256)]
        out = []
        for i, (z, y, x, core) in enumerate(at):
            z, y = move(z, y, core)
            out.append((i, z % 8 * 32 + y % 4 * 8 + x * 2 + core))
        return out

    near_z = lambda z, core: pair(z, core, 8)
    near_y = lambda y, core: pair(y, core, 4)
    far_z = lambda z, core: pair(z // 2, core, 4) * 2 + z % 2
    near = [
        perm(lambda z, y, c: (z, near_y(y, c))),
        perm(lambda z, y, c: (near_z(z, c), y)),
        perm(lambda z, y, c: (near_z(z, c), near_y(y, c))),
    ]
    far = [
        perm(lambda z, y, c: (z, y + 2)),
        perm(lambda z, y, c: (far_z(z, c), y)),
        perm(lambda z, y, c: (far_z(z, c), y + 2)),
    ]
    return near, far, perm(lambda z, y, c: (z + 4, y))


def around_x(value):
    got = {0: value}
    for d in (2, 1, 3):
        got[d] = lax.ppermute(value, "x", [(i, (i + d) % 4) for i in range(4)])
    return [got[d] for d in range(4)]


def swap_core(value):
    return lax.ppermute(value, "core", [(0, 1), (1, 0)])


def local(mom_square, grad_square, basis_square, mom_narrow, grad_narrow, basis_narrow):
    zh, yh = lax.axis_index("zh"), lax.axis_index("yh")
    a, b = zh // 2, zh % 2
    q = lax.axis_index("zl") * 2 + lax.axis_index("yl")
    place = jnp.stack([lax.axis_index("core"), lax.axis_index("x"), q, b, yh]).astype(jnp.int32)
    near, far, across = partners()
    send = lambda value, pairs: lax.ppermute(value, AXES, pairs)
    spread = lambda value, axes, n: lax.all_to_all(jnp.broadcast_to(value[None], (n,) + value.shape), axes, 0, 0)
    inputs = (mom_square, grad_square, basis_square, mom_narrow, grad_narrow, basis_narrow)

    buffers = (mom_square, grad_square, mom_narrow, grad_narrow)
    fetched = [pltpu.VMEM(v.shape, v.dtype) for v in buffers] + [pltpu.SemaphoreType.DMA((4,))]

    mine, theirs = call(
        project_kernel,
        [((4, 4, 32, RANK), F32)] * 2,
        (place,) + inputs,
        [pltpu.VMEM((4, 256, RANK), F32)]
        + [pltpu.VMEM(v.shape, v.dtype) for v in inputs]
        + [pltpu.SemaphoreType.DMA((6, 2))],
        name="project",
        far_in=range(1, 7),
    )
    half = mine + swap_core(theirs)
    part = jnp.sum(lax.all_to_all(half, "x", 0, 0), axis=0)
    own_half = spread(part, "x", 4)
    other_half = swap_core(own_half)

    left, own, *others = call(
        back_kernel,
        [((4, 256, RANK), F32)] + [((8 * CHUNK + 32, RANK), F32)] * 4,
        (place,) + buffers + (own_half, other_half),
        [pltpu.VMEM((32, CHUNK, RANK), F32), pltpu.VMEM((128, RANK), F32)] + fetched,
        name="back",
        far_in=range(1, 5),
    )
    got = [send(value, pairs) for value, pairs in zip(others, near)]
    mine, *others = call(meet_kernel, [((2 * CHUNK + 32, RANK), F32)] * 4, (place, own, *got), name="meet")
    got = [send(value, pairs) for value, pairs in zip(others, far)]
    own = mine + got[0] + got[1] + got[2]
    part = lambda i: jnp.concatenate([lax.dynamic_slice(own, (i * CHUNK, 0), (CHUNK, RANK)), own[2 * CHUNK:]])
    own = part(a) + send(part(1 - a), across)
    own, gram = own[:CHUNK], own[CHUNK:]
    got = send(own, across)
    other_gram = swap_core(gram)
    gram = jnp.where(place[0] == 0, jnp.stack([gram, other_gram]), jnp.stack([other_gram, gram]))
    grams = [gram] + [send(gram, pairs) for pairs in near]
    grams, got = lax.optimization_barrier((grams, got))
    (blocks,) = call(
        factor_kernel,
        [((3, 128, 128), F32)],
        (place, *grams),
        [pltpu.VMEM((RANK, 2 * RANK), F32)],
        name="factor",
    )
    pair = jnp.where(a == 0, jnp.stack([own, got]), jnp.stack([got, own]))
    pairs = [pair] + [send(pair, p) for p in far]
    blocks, pairs = lax.optimization_barrier((blocks, pairs))
    (quarter,) = call(arrange_kernel, [((8, CHUNK, RANK), F32)], (place, *pairs), name="arrange")
    quarters = [quarter] + [send(quarter, p) for p in near]
    around = around_x(blocks)
    inverse = pltpu.VMEM((4, RANK, RANK), F32)
    right_s, right_n, squares = call(
        right_kernel,
        [((2, 1024, RANK), F32), ((2, 128, RANK), F32), ((8, RANK), F32)],
        (place, *quarters, *around),
        [inverse],
        name="right",
    )
    squares, left = lax.optimization_barrier((squares + swap_core(squares), left))
    four_squares = around_x(squares)
    ortho, new_mom_s, new_mom_n = call(
        momentum_kernel,
        [((4, 256, RANK), F32), (mom_square.shape, F32), (mom_narrow.shape, F32)],
        (place, *around, right_s, right_n, left) + buffers,
        [inverse, pltpu.VMEM(mom_square.shape, F32), pltpu.VMEM(mom_narrow.shape, F32), pltpu.SemaphoreType.DMA((4,))],
        name="momentum",
        far_out=(1, 2),
    )
    outs = [(mom_square.shape, BF16), (basis_square.shape, F32), (mom_narrow.shape, BF16), (basis_narrow.shape, F32)]
    up_s, basis_s, up_n, basis_n = call(
        update_kernel,
        outs,
        (place, *four_squares, right_s, right_n, ortho),
        [pltpu.VMEM(*v) for v in outs] + [pltpu.SemaphoreType.DMA((2, 4))],
        name="update",
        far_out=range(4),
    )
    return new_mom_s, up_s, basis_s, new_mom_n, up_n, basis_n


def solution(mesh):
    fine = Mesh(mesh.devices.reshape(4, 2, 2, 2, 4, 2), AXES)
    matrix, factor = P(None, ROWS, COLS), P(None, COLS, None)
    return jax.shard_map(
        local,
        mesh=fine,
        in_specs=(matrix, matrix, factor) * 2,
        out_specs=(matrix, matrix, factor) * 2,
        check_vma=False,
    )
```

```python
import functools

import jax
import jax.numpy as jnp
from jax import lax
from jax.experimental import pallas as pl
from jax.experimental.pallas import tpu as pltpu
from jax.sharding import Mesh, PartitionSpec as P

D = 8192
KVW = 1024
RANK = 256

F32 = jnp.float32
BF16 = jnp.bfloat16
AXES = ("zh", "zl", "yh", "yl", "x", "core")
ROWS = ("zh", "zl", "yh", "yl")
COLS = ("x", "core")
NN = (((1,), (0,)), ((), ()))
NT = (((1,), (1,)), ((), ()))
TN = (((0,), (0,)), ((), ()))
SQ, NA = 32, 8
CHUNK = 2 * SQ + NA


def split(value):
    high = value.astype(BF16)
    return high, (value - high.astype(F32)).astype(BF16)


def dot3(left, right, dims):
    (lh, ll), (rh, rl) = left, right
    dot = functools.partial(lax.dot_general, dimension_numbers=dims, preferred_element_type=F32)
    return dot(lh, rh) + (dot(lh, rl) + dot(ll, rh))


def call(kernel, outs, operands, scratch=(), name=None, far_in=(), far_out=()):
    vmem, hbm = pl.BlockSpec(memory_space=pltpu.VMEM), pl.BlockSpec(memory_space=pltpu.HBM)
    return pl.pallas_call(
        kernel,
        out_shape=[jax.ShapeDtypeStruct(s, d) for s, d in outs],
        in_specs=[pl.BlockSpec(memory_space=pltpu.SMEM)]
        + [hbm if i in far_in else vmem for i in range(1, len(operands))],
        out_specs=[hbm if i in far_out else vmem for i in range(len(outs))],
        scratch_shapes=list(scratch),
        compiler_params=pltpu.CompilerParams(vmem_limit_bytes=20 * 2**20),
        name=name,
    )(*[pltpu.with_memory_space_constraint(a, pltpu.HBM) if i in far_in else a for i, a in enumerate(operands)])


def project_kernel(place, ms, gs, qs, mn, gn, qn, mine, theirs, left, m_in, g_in, q_in, mn_in, gn_in, qn_in, sem):
    core = place[0]
    copies = [
        [pltpu.make_async_copy(a.at[k], b.at[k], sem.at[i, k])
         for i, (a, b) in enumerate(((ms, m_in), (gs, g_in), (qs, q_in)))]
        for k in range(2)
    ]
    copies.append([
        pltpu.make_async_copy(a, b, sem.at[3 + i, 0])
        for i, (a, b) in enumerate(((mn, mn_in), (gn, gn_in), (qn, qn_in)))
    ])
    for group in copies:
        for copy in group:
            copy.start()
    for k in range(4):
        if k < 3:
            for copy in copies[k]:
                copy.wait()
        m, g, q = (m_in, g_in, q_in) if k < 2 else (mn_in, gn_in, qn_in)
        buffer = split(m[k % 2] + g[k % 2].astype(F32))
        left[k] = dot3(buffer, split(q[k % 2]), NN)
    for x in range(4):
        for k in range(4):
            mine[x, k] = left[k, pl.ds(pl.multiple_of(core * 128 + x * 32, 32), 32), :]
            theirs[x, k] = left[k, pl.ds(pl.multiple_of((1 - core) * 128 + x * 32, 32), 32), :]


def fetch(sources, targets, sem):
    copies = [pltpu.make_async_copy(a, b, sem.at[i]) for i, (a, b) in enumerate(zip(sources, targets))]
    for copy in copies:
        copy.start()
    return copies


def prepare_kernel(place, ms, gs, mn, gn, high_s, low_s, high_n, low_n, ms_in, gs_in, mn_in, gn_in, sem):
    for copy in fetch((ms, gs, mn, gn), (ms_in, gs_in, mn_in, gn_in), sem):
        copy.wait()
    for k in range(4):
        m, g, high, low = (ms_in, gs_in, high_s, low_s) if k < 2 else (mn_in, gn_in, high_n, low_n)
        high[k % 2], low[k % 2] = split((m[k % 2] + g[k % 2].astype(F32)).T)


def back_kernel(place, high_s, low_s, high_n, low_n, own_half, other_half, left, own, to_y, to_z, to_d, w, gram):
    core, x, q = place[0], place[1], place[2]
    for i in range(4):
        at = ((x - i) & 3) * 32
        for k in range(4):
            left[k, pl.ds(pl.multiple_of(core * 128 + at, 32), 32), :] = own_half[i, k]
            left[k, pl.ds(pl.multiple_of((1 - core) * 128 + at, 32), 32), :] = other_half[i, k]
    half = left[x, :, pl.ds(pl.multiple_of(core * 128, 128), 128)]
    gram[...] = dot3(split(half), split(left[x]), TN)
    for k in range(2):
        w[:, k * SQ:(k + 1) * SQ, :] = dot3((high_s[k], low_s[k]), split(left[k]), NN).reshape(32, SQ, RANK)
    for k in range(2):
        w[k * 16:(k + 1) * 16, 2 * SQ:, :] = dot3((high_n[k], low_n[k]), split(left[2 + k]), NN).reshape(16, NA, RANK)
    for j, out in enumerate((own, to_y, to_z, to_d)):
        out[:8 * CHUNK] = w[pl.ds((q ^ j) * 8, 8)].reshape(8 * CHUNK, RANK)
        out[8 * CHUNK:] = gram[pl.ds(pl.multiple_of((q ^ j) * 32, 32), 32), :]


def meet_kernel(place, own, r0, r1, r2, mine, to_y, to_z, to_d):
    b, yh = place[3], place[4]
    meet = lambda at: (own[at, :] + r0[at, :]) + (r1[at, :] + r2[at, :])
    gram = meet(slice(8 * CHUNK, None))
    for j, out in enumerate((mine, to_y, to_z, to_d)):
        for a in range(2):
            i = a * 4 + (b ^ (j >> 1)) * 2 + (yh ^ (j & 1))
            out[a * CHUNK:(a + 1) * CHUNK] = meet(pl.ds(pl.multiple_of(i * CHUNK, CHUNK), CHUNK))
        out[2 * CHUNK:] = gram


def stack_kernel(place, a0, a1, a2, a3, out):
    for i, a in enumerate((a0, a1, a2, a3)):
        out[i] = a[...]


def stack(place, arrays):
    return call(stack_kernel, [((4,) + arrays[0].shape, F32)], (place, *arrays), name="stack")


def factor_kernel(place, own_half, other_half, out, w):
    n, nb, step = RANK, 64, 8
    core, q = place[0], place[2]
    for j in range(4):
        w[pl.ds(pl.multiple_of(core * 128 + (q ^ j) * 32, 32), 32), :n] = own_half[j]
        w[pl.ds(pl.multiple_of((1 - core) * 128 + (q ^ j) * 32, 32), 32), :n] = other_half[j]
    row = lax.broadcasted_iota(jnp.int32, (n, n), 0)
    col = lax.broadcasted_iota(jnp.int32, (n, n), 1)
    w[:, n:] = jnp.where(row == col, 1.0, 0.0)
    sub = lax.broadcasted_iota(jnp.int32, (nb, 128), 0)
    for o in range(0, n, nb):
        lo, hi = o // 128 * 128, n + (o + nb + 127) // 128 * 128
        r = [w[o:o + nb, t:t + 128] for t in range(lo, hi, 128)]
        d = jnp.ones((nb, 128), F32)
        for i in range(0, nb, step):
            c = o - lo + i
            cols = [jnp.broadcast_to(r[0][:, c + j:c + j + 1], (nb, 128)) for j in range(step)]
            rows = [[a[i + j:i + j + 1, :] for a in r] for j in range(step)]
            for j in range(step):
                p = i + j
                pivot = cols[j][p:p + 1, :]
                d = jnp.where(sub == p, pivot, d)
                f = jnp.where(sub > p, cols[j] * (1.0 / pivot), 0.0)
                for t in range(j + 1, step):
                    cols[t] = cols[t] - f * cols[t][p:p + 1, :]
                    ft = f[i + t:i + t + 1, :]
                    rows[t] = [a - ft * b for a, b in zip(rows[t], rows[j])]
                r = [a - f * b for a, b in zip(r, rows[j])]
        scale = lax.rsqrt(d)
        s = jnp.concatenate([a * scale for a in r], axis=1)
        half, at = o // 128, o % 128
        out[half, at:at + nb, :] = s[:, n - lo:n - lo + 128]
        if half:
            out[2, at:at + nb, :] = s[:, n - lo + 128:n - lo + 256]
        if o + nb < n:
            change = lax.dot_general(
                s[:, :n - lo], s, TN, precision=lax.Precision.HIGHEST, preferred_element_type=F32
            )
            w[o + nb:, lo:hi] = w[o + nb:, lo:hi] - change[o + nb - lo:]


def fill_inverse(inv, place, around):
    for d, blocks in enumerate(around):
        k = (place[1] - d) & 3
        inv[k, :128, :128] = blocks[0]
        inv[k, :128, 128:] = jnp.zeros((128, 128), F32)
        inv[k, 128:, :128] = blocks[1]
        inv[k, 128:, 128:] = blocks[2]


def arrange_kernel(place, w0, w1, w2, w3, out):
    for j, pair in enumerate((w0, w1, w2, w3)):
        for a in range(2):
            out[a * 4 + (place[3] ^ (j >> 1)) * 2 + (place[4] ^ (j & 1))] = pair[a]


def right_kernel(place, w0, w1, w2, w3, l0, l1, l2, l3, right_s, right_n, squares, inv):
    q = place[2]
    fill_inverse(inv, place, (l0, l1, l2, l3))
    for j, w in enumerate((w0, w1, w2, w3)):
        p = q ^ j
        for k in range(2):
            rows = split(w[:, k * SQ:(k + 1) * SQ, :].reshape(8 * SQ, RANK))
            right_s[k, pl.ds(pl.multiple_of(p * 8 * SQ, 8 * SQ), 8 * SQ), :] = dot3(rows, split(inv[k]), NT)
        rows = split(w[:, 2 * SQ:, :].reshape(8 * NA, RANK))
        right_n[p >> 1, pl.ds(pl.multiple_of((p & 1) * 8 * NA, 8 * NA), 8 * NA), :] = dot3(
            rows, split(inv[2 + (p >> 1)]), NT
        )
    squares[...] = jnp.zeros_like(squares)
    for k in range(4):
        r = (right_s if k < 2 else right_n)[k % 2]
        squares[k:k + 1, :] = jnp.sum(r * r, axis=0, keepdims=True)


def momentum_kernel(place, l0, l1, l2, l3, right_s, right_n, left, ms, gs, mn, gn, ortho, mom_s, mom_n, inv, s_out, n_out, sem):
    fill_inverse(inv, place, (l0, l1, l2, l3))
    copies = []
    for k in range(4):
        m, g, right, mom, new = (ms, gs, right_s, mom_s, s_out) if k < 2 else (mn, gn, right_n, mom_n, n_out)
        o = dot3(split(left[k]), split(inv[k]), NT)
        ortho[k] = o
        low_rank = lax.dot_general(o.astype(BF16), right[k % 2].astype(BF16), NT, preferred_element_type=F32)
        new[k % 2] = (m[k % 2] + g[k % 2].astype(F32)) - (1.0 - 0.95) * low_rank
        copies.append(pltpu.make_async_copy(new.at[k % 2], mom.at[k % 2], sem.at[k]))
        copies[k].start()
    for copy in copies:
        copy.wait()


def update_kernel(place, q0, q1, q2, q3, right_s, right_n, ortho, up_s, basis_s, up_n, basis_n,
                  us_out, bs_out, un_out, bn_out, sem):
    scale = lax.rsqrt((q0[...] + q1[...]) + (q2[...] + q3[...]) + 1e-06)
    copies = []
    for k in range(4):
        right, up, basis, columns, u_out, b_out = (
            (right_s, up_s, basis_s, D, us_out, bs_out) if k < 2 else (right_n, up_n, basis_n, KVW, un_out, bn_out)
        )
        s = scale[k:k + 1, :]
        r = right[k % 2]
        b_out[k % 2] = r * s
        copies.append(pltpu.make_async_copy(b_out.at[k % 2], basis.at[k % 2], sem.at[0, k]))
        copies[-1].start()
        o = ortho[k] * (s * (D * columns / RANK) ** 0.5)
        u_out[k % 2] = dot3(split(o), split(r), NT).astype(BF16)
        copies.append(pltpu.make_async_copy(u_out.at[k % 2], up.at[k % 2], sem.at[1, k]))
        copies[-1].start()
    for copy in copies:
        copy.wait()


def partners():
    def pair(i, core, n):
        return ((i - core) % n ^ 1) + core

    def perm(move):
        at = [(i // 32, i // 8 % 4, i // 2 % 4, i % 2) for i in range(256)]
        out = []
        for i, (z, y, x, core) in enumerate(at):
            z, y = move(z, y, core)
            out.append((i, z % 8 * 32 + y % 4 * 8 + x * 2 + core))
        return out

    near_z = lambda z, core: pair(z, core, 8)
    near_y = lambda y, core: pair(y, core, 4)
    far_z = lambda z, core: pair(z // 2, core, 4) * 2 + z % 2
    near = [
        perm(lambda z, y, c: (z, near_y(y, c))),
        perm(lambda z, y, c: (near_z(z, c), y)),
        perm(lambda z, y, c: (near_z(z, c), near_y(y, c))),
    ]
    far = [
        perm(lambda z, y, c: (z, y + 2)),
        perm(lambda z, y, c: (far_z(z, c), y)),
        perm(lambda z, y, c: (far_z(z, c), y + 2)),
    ]
    return near, far, perm(lambda z, y, c: (z + 4, y))


def shift_x(value, d):
    return lax.ppermute(value, "x", [(i, (i + d) % 4) for i in range(4)])


def around_x(value):
    got = {0: value}
    for d in (2, 1, 3):
        got[d] = shift_x(value, d)
    return [got[d] for d in range(4)]


def swap_core(value):
    return lax.ppermute(value, "core", [(0, 1), (1, 0)])


def local(mom_square, grad_square, basis_square, mom_narrow, grad_narrow, basis_narrow):
    zh, yh = lax.axis_index("zh"), lax.axis_index("yh")
    a, b = zh // 2, zh % 2
    q = lax.axis_index("zl") * 2 + lax.axis_index("yl")
    place = jnp.stack([lax.axis_index("core"), lax.axis_index("x"), q, b, yh]).astype(jnp.int32)
    near, far, across = partners()
    send = lambda value, pairs: lax.ppermute(value, AXES, pairs)
    inputs = (mom_square, grad_square, basis_square, mom_narrow, grad_narrow, basis_narrow)

    buffers = (mom_square, grad_square, mom_narrow, grad_narrow)
    fetched = [pltpu.VMEM(v.shape, v.dtype) for v in buffers] + [pltpu.SemaphoreType.DMA((4,))]

    mine, theirs = call(
        project_kernel,
        [((4, 4, 32, RANK), F32)] * 2,
        (place,) + inputs,
        [pltpu.VMEM((4, 256, RANK), F32)]
        + [pltpu.VMEM(v.shape, v.dtype) for v in inputs]
        + [pltpu.SemaphoreType.DMA((6, 2))],
        name="project",
        far_in=range(1, 7),
    )
    half = mine + swap_core(theirs)
    chunks = [lax.dynamic_index_in_dim(half, (lax.axis_index("x") + d) % 4, 0, keepdims=False) for d in range(4)]
    chunks, buffers_late = lax.optimization_barrier((chunks, buffers))
    got = [shift_x(chunks[d], d) for d in (2, 1, 3)]
    transposes = call(
        prepare_kernel,
        [(v, BF16) for v in ((2, 1024, 256),) * 2 + ((2, 128, 256),) * 2],
        (place,) + buffers_late,
        fetched,
        name="prepare",
        far_in=range(1, 5),
    )
    got, transposes = lax.optimization_barrier((got, transposes))
    own_half = jnp.stack(around_x((chunks[0] + got[0]) + (got[1] + got[2])))
    other_half = swap_core(own_half)

    left, own, *others = call(
        back_kernel,
        [((4, 256, RANK), F32)] + [((8 * CHUNK + 32, RANK), F32)] * 4,
        (place, *transposes, own_half, other_half),
        [pltpu.VMEM((32, CHUNK, RANK), F32), pltpu.VMEM((128, RANK), F32)],
        name="back",
    )
    got = [send(value, pairs) for value, pairs in zip(others[::-1], near[::-1])][::-1]
    mine, *others = call(meet_kernel, [((2 * CHUNK + 32, RANK), F32)] * 4, (place, own, *got), name="meet")
    got = [send(value, pairs) for value, pairs in zip(others[::-1], far[::-1])][::-1]
    own = mine + got[0] + got[1] + got[2]
    part = lambda i: jnp.concatenate([lax.dynamic_slice(own, (i * CHUNK, 0), (CHUNK, RANK)), own[2 * CHUNK:]])
    own = part(a) + send(part(1 - a), across)
    own, gram = own[:CHUNK], own[CHUNK:]
    got = send(own, across)
    (gram,) = stack(place, [gram] + [send(gram, pairs) for pairs in near])
    gram, got = lax.optimization_barrier((gram, got))
    other_gram = swap_core(gram)
    (blocks,) = call(
        factor_kernel,
        [((3, 128, 128), F32)],
        (place, gram, other_gram),
        [pltpu.VMEM((RANK, 2 * RANK), F32)],
        name="factor",
    )
    pair = jnp.where(a == 0, jnp.stack([own, got]), jnp.stack([got, own]))
    pairs = [pair] + [send(pair, p) for p in far]
    blocks, pairs = lax.optimization_barrier((blocks, pairs))
    (quarter,) = call(arrange_kernel, [((8, CHUNK, RANK), F32)], (place, *pairs), name="arrange")
    quarters = [quarter] + [send(quarter, p) for p in near]
    around = around_x(blocks)
    inverse = pltpu.VMEM((4, RANK, RANK), F32)
    right_s, right_n, squares = call(
        right_kernel,
        [((2, 1024, RANK), F32), ((2, 128, RANK), F32), ((8, RANK), F32)],
        (place, *quarters, *around),
        [inverse],
        name="right",
    )
    squares, left = lax.optimization_barrier((squares + swap_core(squares), left))
    four_squares = around_x(squares)
    ortho, new_mom_s, new_mom_n = call(
        momentum_kernel,
        [((4, 256, RANK), F32), (mom_square.shape, F32), (mom_narrow.shape, F32)],
        (place, *around, right_s, right_n, left) + buffers,
        [inverse, pltpu.VMEM(mom_square.shape, F32), pltpu.VMEM(mom_narrow.shape, F32), pltpu.SemaphoreType.DMA((4,))],
        name="momentum",
        far_out=(1, 2),
    )
    outs = [(mom_square.shape, BF16), (basis_square.shape, F32), (mom_narrow.shape, BF16), (basis_narrow.shape, F32)]
    up_s, basis_s, up_n, basis_n = call(
        update_kernel,
        outs,
        (place, *four_squares, right_s, right_n, ortho),
        [pltpu.VMEM(*v) for v in outs] + [pltpu.SemaphoreType.DMA((2, 4))],
        name="update",
        far_out=range(4),
    )
    return new_mom_s, up_s, basis_s, new_mom_n, up_n, basis_n


def solution(mesh):
    fine = Mesh(mesh.devices.reshape(4, 2, 2, 2, 4, 2), AXES)
    matrix, factor = P(None, ROWS, COLS), P(None, COLS, None)
    return jax.shard_map(
        local,
        mesh=fine,
        in_specs=(matrix, matrix, factor) * 2,
        out_specs=(matrix, matrix, factor) * 2,
        check_vma=False,
    )
```

```python
import functools

import jax
import jax.numpy as jnp
from jax import lax
from jax.experimental import pallas as pl
from jax.experimental.pallas import tpu as pltpu
from jax.sharding import Mesh, PartitionSpec as P

D = 8192
KVW = 1024
RANK = 256

F32 = jnp.float32
BF16 = jnp.bfloat16
AXES = ("zh", "zl", "yh", "yl", "x", "core")
ROWS = ("zh", "zl", "yh", "yl")
COLS = ("x", "core")
NN = (((1,), (0,)), ((), ()))
NT = (((1,), (1,)), ((), ()))
TN = (((0,), (0,)), ((), ()))
SQ, NA = 32, 8
CHUNK = 2 * SQ + NA


def split(value):
    high = value.astype(BF16)
    return high, (value - high.astype(F32)).astype(BF16)


def dot3(left, right, dims):
    (lh, ll), (rh, rl) = left, right
    dot = functools.partial(lax.dot_general, dimension_numbers=dims, preferred_element_type=F32)
    return dot(lh, rh) + (dot(lh, rl) + dot(ll, rh))


def call(kernel, outs, operands, scratch=(), name=None, far_in=(), far_out=()):
    vmem, hbm = pl.BlockSpec(memory_space=pltpu.VMEM), pl.BlockSpec(memory_space=pltpu.HBM)
    return pl.pallas_call(
        kernel,
        out_shape=[jax.ShapeDtypeStruct(s, d) for s, d in outs],
        in_specs=[pl.BlockSpec(memory_space=pltpu.SMEM)]
        + [hbm if i in far_in else vmem for i in range(1, len(operands))],
        out_specs=[hbm if i in far_out else vmem for i in range(len(outs))],
        scratch_shapes=list(scratch),
        compiler_params=pltpu.CompilerParams(vmem_limit_bytes=20 * 2**20),
        name=name,
    )(*[pltpu.with_memory_space_constraint(a, pltpu.HBM) if i in far_in else a for i, a in enumerate(operands)])


def project_kernel(place, ms, gs, qs, mn, gn, qn, mine, theirs, left, m_in, g_in, q_in, mn_in, gn_in, qn_in, sem):
    core = place[0]
    copies = [
        [pltpu.make_async_copy(a.at[k], b.at[k], sem.at[i, k])
         for i, (a, b) in enumerate(((ms, m_in), (gs, g_in), (qs, q_in)))]
        for k in range(2)
    ]
    copies.append([
        pltpu.make_async_copy(a, b, sem.at[3 + i, 0])
        for i, (a, b) in enumerate(((mn, mn_in), (gn, gn_in), (qn, qn_in)))
    ])
    for group in copies:
        for copy in group:
            copy.start()
    for k in range(4):
        if k < 3:
            for copy in copies[k]:
                copy.wait()
        m, g, q = (m_in, g_in, q_in) if k < 2 else (mn_in, gn_in, qn_in)
        buffer = split(m[k % 2] + g[k % 2].astype(F32))
        left[k] = dot3(buffer, split(q[k % 2]), NN)
    for x in range(4):
        for k in range(4):
            mine[x, k] = left[k, pl.ds(pl.multiple_of(core * 128 + x * 32, 32), 32), :]
            theirs[x, k] = left[k, pl.ds(pl.multiple_of((1 - core) * 128 + x * 32, 32), 32), :]


def fetch(sources, targets, sem):
    copies = [pltpu.make_async_copy(a, b, sem.at[i]) for i, (a, b) in enumerate(zip(sources, targets))]
    for copy in copies:
        copy.start()
    return copies


def prepare_kernel(place, ms, gs, mn, gn, high_s, low_s, high_n, low_n, ms_in, gs_in, mn_in, gn_in, sem):
    for copy in fetch((ms, gs, mn, gn), (ms_in, gs_in, mn_in, gn_in), sem):
        copy.wait()
    for k in range(4):
        m, g, high, low = (ms_in, gs_in, high_s, low_s) if k < 2 else (mn_in, gn_in, high_n, low_n)
        high[k % 2], low[k % 2] = split((m[k % 2] + g[k % 2].astype(F32)).T)


def back_kernel(place, high_s, low_s, high_n, low_n, own_half, other_half, left, own, to_y, to_z, to_d, w, gram):
    core, x, q = place[0], place[1], place[2]
    for i in range(4):
        at = ((x - i) & 3) * 32
        for k in range(4):
            left[k, pl.ds(pl.multiple_of(core * 128 + at, 32), 32), :] = own_half[i, k]
            left[k, pl.ds(pl.multiple_of((1 - core) * 128 + at, 32), 32), :] = other_half[i, k]
    half = left[x, :, pl.ds(pl.multiple_of(core * 128, 128), 128)]
    gram[...] = dot3(split(half), split(left[x]), TN)
    for k in range(2):
        w[:, k * SQ:(k + 1) * SQ, :] = dot3((high_s[k], low_s[k]), split(left[k]), NN).reshape(32, SQ, RANK)
    for k in range(2):
        w[k * 16:(k + 1) * 16, 2 * SQ:, :] = dot3((high_n[k], low_n[k]), split(left[2 + k]), NN).reshape(16, NA, RANK)
    for j, out in enumerate((own, to_y, to_z, to_d)):
        out[:8 * CHUNK] = w[pl.ds((q ^ j) * 8, 8)].reshape(8 * CHUNK, RANK)
        out[8 * CHUNK:] = gram[pl.ds(pl.multiple_of((q ^ j) * 32, 32), 32), :]


def meet_kernel(place, own, r0, r1, r2, mine, to_y, to_z, to_d):
    b, yh = place[3], place[4]
    meet = lambda at: (own[at, :] + r0[at, :]) + (r1[at, :] + r2[at, :])
    gram = meet(slice(8 * CHUNK, None))
    for j, out in enumerate((mine, to_y, to_z, to_d)):
        for a in range(2):
            i = a * 4 + (b ^ (j >> 1)) * 2 + (yh ^ (j & 1))
            out[a * CHUNK:(a + 1) * CHUNK] = meet(pl.ds(pl.multiple_of(i * CHUNK, CHUNK), CHUNK))
        out[2 * CHUNK:] = gram


def stack_kernel(place, a0, a1, a2, a3, out):
    for i, a in enumerate((a0, a1, a2, a3)):
        out[i] = a[...]


def stack(place, arrays):
    return call(stack_kernel, [((4,) + arrays[0].shape, F32)], (place, *arrays), name="stack")


def eliminate(w, base, start, stop, write):
    n, nb, step = RANK, 64, 8
    sub = lax.broadcasted_iota(jnp.int32, (nb, 128), 0)
    for o in range(start, stop, nb):
        lo, hi = o // 128 * 128, n + (o + nb + 127) // 128 * 128
        r = [w[o - base:o - base + nb, t:t + 128] for t in range(lo, hi, 128)]
        d = jnp.ones((nb, 128), F32)
        for i in range(0, nb, step):
            c = o - lo + i
            cols = [jnp.broadcast_to(r[0][:, c + j:c + j + 1], (nb, 128)) for j in range(step)]
            rows = [[a[i + j:i + j + 1, :] for a in r] for j in range(step)]
            for j in range(step):
                p = i + j
                pivot = cols[j][p:p + 1, :]
                d = jnp.where(sub == p, pivot, d)
                f = jnp.where(sub > p, cols[j] * (1.0 / pivot), 0.0)
                for t in range(j + 1, step):
                    cols[t] = cols[t] - f * cols[t][p:p + 1, :]
                    ft = f[i + t:i + t + 1, :]
                    rows[t] = [a - ft * b for a, b in zip(rows[t], rows[j])]
                r = [a - f * b for a, b in zip(r, rows[j])]
        scale = lax.rsqrt(d)
        s = jnp.concatenate([a * scale for a in r], axis=1)
        write(o % 128, s[:, n - lo:])
        if o + nb < n:
            change = lax.dot_general(
                s[:, :n - lo], s, TN, precision=lax.Precision.HIGHEST, preferred_element_type=F32
            )
            w[o + nb - base:, lo:hi] = w[o + nb - base:, lo:hi] - change[o + nb - lo:]


def factor_first_kernel(place, own_half, other_half, top, w):
    n, core, q = RANK, place[0], place[2]
    for j in range(4):
        w[pl.ds(pl.multiple_of(core * 128 + (q ^ j) * 32, 32), 32), :n] = own_half[j]
        w[pl.ds(pl.multiple_of((1 - core) * 128 + (q ^ j) * 32, 32), 32), :n] = other_half[j]
    row = lax.broadcasted_iota(jnp.int32, (n, n), 0)
    col = lax.broadcasted_iota(jnp.int32, (n, n), 1)
    w[:, n:] = jnp.where(row == col, 1.0, 0.0)

    def write(at, s):
        top[at:at + s.shape[0], :] = s

    eliminate(w, 0, 0, 128, write)


def factor_second_kernel(place, top, rest, out, out_half, w):
    w[...] = rest[128:, :]
    out[0] = top[...]

    def write(at, s):
        out[1, at:at + s.shape[0], :] = s[:, :128]
        out[2, at:at + s.shape[0], :] = s[:, 128:]

    eliminate(w, 128, 128, 256, write)
    out_half[...] = out[:, pl.ds(pl.multiple_of(place[0] * 64, 64), 64), :]


def fill_inverse(inv, place, around):
    core, x = place[0], place[1]
    inv[:, :128, 128:] = jnp.zeros((4, 128, 128), F32)

    def fill(k, blocks, at, size):
        for i, (row, col) in enumerate(((0, 0), (128, 0), (128, 128))):
            inv[k, pl.ds(pl.multiple_of(row + at, 64), size), col:col + 128] = blocks[i]

    own, near, other_near, far, other_far = around
    fill(x, own, 0, 128)
    fill((x + 2 * core - 1) & 3, near, 0, 128)
    fill((x - 2 * core + 1) & 3, other_near, 0, 128)
    fill((x + 2) & 3, far, core * 64, 64)
    fill((x + 2) & 3, other_far, (1 - core) * 64, 64)


def arrange_kernel(place, w0, w1, w2, w3, out):
    for j, pair in enumerate((w0, w1, w2, w3)):
        for a in range(2):
            out[a * 4 + (place[3] ^ (j >> 1)) * 2 + (place[4] ^ (j & 1))] = pair[a]


def right_kernel(place, w0, w1, w2, w3, l0, l1, l2, l3, l4, right_s, right_n, squares, inv):
    q = place[2]
    fill_inverse(inv, place, (l0, l1, l2, l3, l4))
    for j, w in enumerate((w0, w1, w2, w3)):
        p = q ^ j
        for k in range(2):
            rows = split(w[:, k * SQ:(k + 1) * SQ, :].reshape(8 * SQ, RANK))
            right_s[k, pl.ds(pl.multiple_of(p * 8 * SQ, 8 * SQ), 8 * SQ), :] = dot3(rows, split(inv[k]), NT)
        rows = split(w[:, 2 * SQ:, :].reshape(8 * NA, RANK))
        right_n[p >> 1, pl.ds(pl.multiple_of((p & 1) * 8 * NA, 8 * NA), 8 * NA), :] = dot3(
            rows, split(inv[2 + (p >> 1)]), NT
        )
    squares[...] = jnp.zeros_like(squares)
    for k in range(4):
        r = (right_s if k < 2 else right_n)[k % 2]
        squares[k:k + 1, :] = jnp.sum(r * r, axis=0, keepdims=True)


def momentum_kernel(place, l0, l1, l2, l3, l4, right_s, right_n, left, ms, gs, mn, gn, ortho, mom_s, mom_n, inv, s_out, n_out, sem):
    fill_inverse(inv, place, (l0, l1, l2, l3, l4))
    copies = []
    for k in range(4):
        m, g, right, mom, new = (ms, gs, right_s, mom_s, s_out) if k < 2 else (mn, gn, right_n, mom_n, n_out)
        o = dot3(split(left[k]), split(inv[k]), NT)
        ortho[k] = o
        low_rank = lax.dot_general(o.astype(BF16), right[k % 2].astype(BF16), NT, preferred_element_type=F32)
        new[k % 2] = (m[k % 2] + g[k % 2].astype(F32)) - (1.0 - 0.95) * low_rank
        copies.append(pltpu.make_async_copy(new.at[k % 2], mom.at[k % 2], sem.at[k]))
        copies[k].start()
    for copy in copies:
        copy.wait()


def update_kernel(place, q0, q1, q2, q3, right_s, right_n, ortho, up_s, basis_s, up_n, basis_n,
                  us_out, bs_out, un_out, bn_out, sem):
    scale = lax.rsqrt((q0[...] + q1[...]) + (q2[...] + q3[...]) + 1e-06)
    copies = []
    for k in range(4):
        right, up, basis, columns, u_out, b_out = (
            (right_s, up_s, basis_s, D, us_out, bs_out) if k < 2 else (right_n, up_n, basis_n, KVW, un_out, bn_out)
        )
        s = scale[k:k + 1, :]
        r = right[k % 2]
        b_out[k % 2] = r * s
        copies.append(pltpu.make_async_copy(b_out.at[k % 2], basis.at[k % 2], sem.at[0, k]))
        copies[-1].start()
        o = ortho[k] * (s * (D * columns / RANK) ** 0.5)
        u_out[k % 2] = dot3(split(o), split(r), NT).astype(BF16)
        copies.append(pltpu.make_async_copy(u_out.at[k % 2], up.at[k % 2], sem.at[1, k]))
        copies[-1].start()
    for copy in copies:
        copy.wait()


def partners():
    def pair(i, core, n):
        return ((i - core) % n ^ 1) + core

    def perm(move):
        at = [(i // 32, i // 8 % 4, i // 2 % 4, i % 2) for i in range(256)]
        out = []
        for i, (z, y, x, core) in enumerate(at):
            z, y = move(z, y, core)
            out.append((i, z % 8 * 32 + y % 4 * 8 + x * 2 + core))
        return out

    near_z = lambda z, core: pair(z, core, 8)
    near_y = lambda y, core: pair(y, core, 4)
    far_z = lambda z, core: pair(z // 2, core, 4) * 2 + z % 2
    near = [
        perm(lambda z, y, c: (z, near_y(y, c))),
        perm(lambda z, y, c: (near_z(z, c), y)),
        perm(lambda z, y, c: (near_z(z, c), near_y(y, c))),
    ]
    far = [
        perm(lambda z, y, c: (z, y + 2)),
        perm(lambda z, y, c: (far_z(z, c), y)),
        perm(lambda z, y, c: (far_z(z, c), y + 2)),
    ]
    sides = [(i, i // 8 * 8 + (i % 8 + (2 if i % 2 == 0 else 6)) % 8) for i in range(256)]
    return near, far, perm(lambda z, y, c: (z + 4, y)), sides


def shift_x(value, d):
    return lax.ppermute(value, "x", [(i, (i + d) % 4) for i in range(4)])


def around_x(value):
    got = {0: value}
    for d in (2, 1, 3):
        got[d] = shift_x(value, d)
    return [got[d] for d in range(4)]


def swap_core(value):
    return lax.ppermute(value, "core", [(0, 1), (1, 0)])


def local(mom_square, grad_square, basis_square, mom_narrow, grad_narrow, basis_narrow):
    zh, yh = lax.axis_index("zh"), lax.axis_index("yh")
    a, b = zh // 2, zh % 2
    q = lax.axis_index("zl") * 2 + lax.axis_index("yl")
    place = jnp.stack([lax.axis_index("core"), lax.axis_index("x"), q, b, yh]).astype(jnp.int32)
    near, far, across, sides = partners()
    send = lambda value, pairs: lax.ppermute(value, AXES, pairs)
    inputs = (mom_square, grad_square, basis_square, mom_narrow, grad_narrow, basis_narrow)

    buffers = (mom_square, grad_square, mom_narrow, grad_narrow)
    fetched = [pltpu.VMEM(v.shape, v.dtype) for v in buffers] + [pltpu.SemaphoreType.DMA((4,))]

    mine, theirs = call(
        project_kernel,
        [((4, 4, 32, RANK), F32)] * 2,
        (place,) + inputs,
        [pltpu.VMEM((4, 256, RANK), F32)]
        + [pltpu.VMEM(v.shape, v.dtype) for v in inputs]
        + [pltpu.SemaphoreType.DMA((6, 2))],
        name="project",
        far_in=range(1, 7),
    )
    half = mine + swap_core(theirs)
    chunks = [lax.dynamic_index_in_dim(half, (lax.axis_index("x") + d) % 4, 0, keepdims=False) for d in range(4)]
    chunks, buffers_late = lax.optimization_barrier((chunks, buffers))
    got = [shift_x(chunks[d], d) for d in (2, 1, 3)]
    transposes = call(
        prepare_kernel,
        [(v, BF16) for v in ((2, 1024, 256),) * 2 + ((2, 128, 256),) * 2],
        (place,) + buffers_late,
        fetched,
        name="prepare",
        far_in=range(1, 5),
    )
    got, transposes = lax.optimization_barrier((got, transposes))
    own_half = jnp.stack(around_x((chunks[0] + got[0]) + (got[1] + got[2])))
    other_half = swap_core(own_half)

    left, own, *others = call(
        back_kernel,
        [((4, 256, RANK), F32)] + [((8 * CHUNK + 32, RANK), F32)] * 4,
        (place, *transposes, own_half, other_half),
        [pltpu.VMEM((32, CHUNK, RANK), F32), pltpu.VMEM((128, RANK), F32)],
        name="back",
    )
    got = [send(value, pairs) for value, pairs in zip(others[::-1], near[::-1])]
    mine, *others = call(meet_kernel, [((2 * CHUNK + 32, RANK), F32)] * 4, (place, own, *got), name="meet")
    got = [send(value, pairs) for value, pairs in zip(others[::-1], far[::-1])][::-1]
    own = mine + got[0] + got[1] + got[2]
    part = lambda i: jnp.concatenate([lax.dynamic_slice(own, (i * CHUNK, 0), (CHUNK, RANK)), own[2 * CHUNK:]])
    own = part(a) + send(part(1 - a), across)
    own, gram = own[:CHUNK], own[CHUNK:]
    got = send(own, across)
    (gram,) = stack(place, [gram] + [send(gram, pairs) for pairs in near])
    gram, got = lax.optimization_barrier((gram, got))
    other_gram = swap_core(gram)
    top, rest = call(
        factor_first_kernel,
        [((128, 128), F32), ((RANK, 2 * RANK), F32)],
        (place, gram, other_gram),
        name="factor_first",
    )
    pair = jnp.where(a == 0, jnp.stack([own, got]), jnp.stack([got, own]))
    pairs = [pair] + [send(pair, p) for p in far]
    top, rest, pairs = lax.optimization_barrier((top, rest, pairs))
    (quarter,) = call(arrange_kernel, [((8, CHUNK, RANK), F32)], (place, *pairs), name="arrange")
    quarters = [quarter] + [send(quarter, p) for p in near]
    blocks, half_blocks = call(
        factor_second_kernel,
        [((3, 128, 128), F32), ((3, 64, 128), F32)],
        (place, top, rest),
        [pltpu.VMEM((128, 2 * RANK), F32)],
        name="factor_second",
    )
    beside, apart = send(blocks, sides), shift_x(half_blocks, 2)
    around = blocks, beside, swap_core(beside), apart, swap_core(apart)
    inverse = pltpu.VMEM((4, RANK, RANK), F32)
    right_s, right_n, squares = call(
        right_kernel,
        [((2, 1024, RANK), F32), ((2, 128, RANK), F32), ((8, RANK), F32)],
        (place, *quarters, *around),
        [inverse],
        name="right",
    )
    squares, left = lax.optimization_barrier((squares + swap_core(squares), left))
    four_squares = around_x(squares)
    ortho, new_mom_s, new_mom_n = call(
        momentum_kernel,
        [((4, 256, RANK), F32), (mom_square.shape, F32), (mom_narrow.shape, F32)],
        (place, *around, right_s, right_n, left) + buffers,
        [inverse, pltpu.VMEM(mom_square.shape, F32), pltpu.VMEM(mom_narrow.shape, F32), pltpu.SemaphoreType.DMA((4,))],
        name="momentum",
        far_out=(1, 2),
    )
    outs = [(mom_square.shape, BF16), (basis_square.shape, F32), (mom_narrow.shape, BF16), (basis_narrow.shape, F32)]
    up_s, basis_s, up_n, basis_n = call(
        update_kernel,
        outs,
        (place, *four_squares, right_s, right_n, ortho),
        [pltpu.VMEM(*v) for v in outs] + [pltpu.SemaphoreType.DMA((2, 4))],
        name="update",
        far_out=range(4),
    )
    return new_mom_s, up_s, basis_s, new_mom_n, up_n, basis_n


def solution(mesh):
    fine = Mesh(mesh.devices.reshape(4, 2, 2, 2, 4, 2), AXES)
    matrix, factor = P(None, ROWS, COLS), P(None, COLS, None)
    return jax.shard_map(
        local,
        mesh=fine,
        in_specs=(matrix, matrix, factor) * 2,
        out_specs=(matrix, matrix, factor) * 2,
        check_vma=False,
    )
```

```python
import functools

import jax
import jax.numpy as jnp
from jax import lax
from jax.experimental import pallas as pl
from jax.experimental.pallas import tpu as pltpu
from jax.sharding import Mesh, PartitionSpec as P

D = 8192
KVW = 1024
RANK = 256

F32 = jnp.float32
BF16 = jnp.bfloat16
AXES = ("zh", "zl", "yh", "yl", "x", "core")
ROWS = ("zh", "zl", "yh", "yl")
COLS = ("x", "core")
NN = (((1,), (0,)), ((), ()))
NT = (((1,), (1,)), ((), ()))
TN = (((0,), (0,)), ((), ()))
SQ, NA = 32, 8
CHUNK = 2 * SQ + NA


def split(value):
    high = value.astype(BF16)
    return high, (value - high.astype(F32)).astype(BF16)


def dot3(left, right, dims):
    (lh, ll), (rh, rl) = left, right
    dot = functools.partial(lax.dot_general, dimension_numbers=dims, preferred_element_type=F32)
    return dot(lh, rh) + (dot(lh, rl) + dot(ll, rh))


def call(kernel, outs, operands, scratch=(), name=None, far_in=(), far_out=()):
    vmem, hbm = pl.BlockSpec(memory_space=pltpu.VMEM), pl.BlockSpec(memory_space=pltpu.HBM)
    return pl.pallas_call(
        kernel,
        out_shape=[jax.ShapeDtypeStruct(s, d) for s, d in outs],
        in_specs=[pl.BlockSpec(memory_space=pltpu.SMEM)]
        + [hbm if i in far_in else vmem for i in range(1, len(operands))],
        out_specs=[hbm if i in far_out else vmem for i in range(len(outs))],
        scratch_shapes=list(scratch),
        compiler_params=pltpu.CompilerParams(vmem_limit_bytes=20 * 2**20),
        name=name,
    )(*[pltpu.with_memory_space_constraint(a, pltpu.HBM) if i in far_in else a for i, a in enumerate(operands)])


def project_kernel(place, ms, gs, qs, mn, gn, qn, mine, theirs, left, m_in, g_in, q_in, mn_in, gn_in, qn_in, sem):
    core = place[0]
    copies = [
        [pltpu.make_async_copy(a.at[k], b.at[k], sem.at[i, k])
         for i, (a, b) in enumerate(((ms, m_in), (gs, g_in), (qs, q_in)))]
        for k in range(2)
    ]
    copies.append([
        pltpu.make_async_copy(a, b, sem.at[3 + i, 0])
        for i, (a, b) in enumerate(((mn, mn_in), (gn, gn_in), (qn, qn_in)))
    ])
    for group in copies:
        for copy in group:
            copy.start()
    for k in range(4):
        if k < 3:
            for copy in copies[k]:
                copy.wait()
        m, g, q = (m_in, g_in, q_in) if k < 2 else (mn_in, gn_in, qn_in)
        buffer = split(m[k % 2] + g[k % 2].astype(F32))
        left[k] = dot3(buffer, split(q[k % 2]), NN)
    for x in range(4):
        for k in range(4):
            mine[x, k] = left[k, pl.ds(pl.multiple_of(core * 128 + x * 32, 32), 32), :]
            theirs[x, k] = left[k, pl.ds(pl.multiple_of((1 - core) * 128 + x * 32, 32), 32), :]


def fetch(sources, targets, sem):
    copies = [pltpu.make_async_copy(a, b, sem.at[i]) for i, (a, b) in enumerate(zip(sources, targets))]
    for copy in copies:
        copy.start()
    return copies


def prepare_kernel(place, ms, gs, mn, gn, high_s, low_s, high_n, low_n, ms_in, gs_in, mn_in, gn_in, sem):
    for copy in fetch((ms, gs, mn, gn), (ms_in, gs_in, mn_in, gn_in), sem):
        copy.wait()
    for k in range(4):
        m, g, high, low = (ms_in, gs_in, high_s, low_s) if k < 2 else (mn_in, gn_in, high_n, low_n)
        high[k % 2], low[k % 2] = split((m[k % 2] + g[k % 2].astype(F32)).T)


def back_kernel(place, high_s, low_s, high_n, low_n, h0, h1, h2, h3, o0, o1, o2, o3, left, own, to_y, to_z, to_d, w, gram):
    core, x, q = place[0], place[1], place[2]
    own_half, other_half = (h0, h1, h2, h3), (o0, o1, o2, o3)
    for i in range(4):
        at = ((x - i) & 3) * 32
        for k in range(4):
            left[k, pl.ds(pl.multiple_of(core * 128 + at, 32), 32), :] = own_half[i][k]
            left[k, pl.ds(pl.multiple_of((1 - core) * 128 + at, 32), 32), :] = other_half[i][k]
    half = left[x, :, pl.ds(pl.multiple_of(core * 128, 128), 128)]
    gram[...] = dot3(split(half), split(left[x]), TN)
    for k in range(2):
        w[:, k * SQ:(k + 1) * SQ, :] = dot3((high_s[k], low_s[k]), split(left[k]), NN).reshape(32, SQ, RANK)
    for k in range(2):
        w[k * 16:(k + 1) * 16, 2 * SQ:, :] = dot3((high_n[k], low_n[k]), split(left[2 + k]), NN).reshape(16, NA, RANK)
    for j, out in enumerate((own, to_y, to_z, to_d)):
        out[:8 * CHUNK] = w[pl.ds((q ^ j) * 8, 8)].reshape(8 * CHUNK, RANK)
        out[8 * CHUNK:] = gram[pl.ds(pl.multiple_of((q ^ j) * 32, 32), 32), :]


def meet_kernel(place, own, r0, r1, r2, mine, to_y, to_z, to_d):
    b, yh = place[3], place[4]
    meet = lambda at: (own[at, :] + r0[at, :]) + (r1[at, :] + r2[at, :])
    gram = meet(slice(8 * CHUNK, None))
    for j, out in enumerate((mine, to_y, to_z, to_d)):
        for a in range(2):
            i = a * 4 + (b ^ (j >> 1)) * 2 + (yh ^ (j & 1))
            out[a * CHUNK:(a + 1) * CHUNK] = meet(pl.ds(pl.multiple_of(i * CHUNK, CHUNK), CHUNK))
        out[2 * CHUNK:] = gram


def stack_kernel(place, a0, a1, a2, a3, out):
    for i, a in enumerate((a0, a1, a2, a3)):
        out[i] = a[...]


def stack(place, arrays):
    return call(stack_kernel, [((4,) + arrays[0].shape, F32)], (place, *arrays), name="stack")


def eliminate(w, base, start, stop, write):
    n, nb, step = RANK, 64, 8
    sub = lax.broadcasted_iota(jnp.int32, (nb, 128), 0)
    for o in range(start, stop, nb):
        lo, hi = o // 128 * 128, n + (o + nb + 127) // 128 * 128
        r = [w[o - base:o - base + nb, t:t + 128] for t in range(lo, hi, 128)]
        d = jnp.ones((nb, 128), F32)
        for i in range(0, nb, step):
            c = o - lo + i
            cols = [jnp.broadcast_to(r[0][:, c + j:c + j + 1], (nb, 128)) for j in range(step)]
            rows = [[a[i + j:i + j + 1, :] for a in r] for j in range(step)]
            for j in range(step):
                p = i + j
                pivot = cols[j][p:p + 1, :]
                d = jnp.where(sub == p, pivot, d)
                f = jnp.where(sub > p, cols[j] * (1.0 / pivot), 0.0)
                for t in range(j + 1, step):
                    cols[t] = cols[t] - f * cols[t][p:p + 1, :]
                    ft = f[i + t:i + t + 1, :]
                    rows[t] = [a - ft * b for a, b in zip(rows[t], rows[j])]
                r = [a - f * b for a, b in zip(r, rows[j])]
        scale = lax.rsqrt(d)
        s = jnp.concatenate([a * scale for a in r], axis=1)
        write(o % 128, s[:, n - lo:])
        if o + nb < n:
            change = lax.dot_general(
                s[:, :n - lo], s, TN, precision=lax.Precision.HIGHEST, preferred_element_type=F32
            )
            w[o + nb - base:, lo:hi] = w[o + nb - base:, lo:hi] - change[o + nb - lo:]


def factor_first_kernel(place, own_half, other_half, top, w):
    n, core, q = RANK, place[0], place[2]
    for j in range(4):
        w[pl.ds(pl.multiple_of(core * 128 + (q ^ j) * 32, 32), 32), :n] = own_half[j]
        w[pl.ds(pl.multiple_of((1 - core) * 128 + (q ^ j) * 32, 32), 32), :n] = other_half[j]
    row = lax.broadcasted_iota(jnp.int32, (n, n), 0)
    col = lax.broadcasted_iota(jnp.int32, (n, n), 1)
    w[:, n:] = jnp.where(row == col, 1.0, 0.0)

    def write(at, s):
        top[at:at + s.shape[0], :] = s

    eliminate(w, 0, 0, 128, write)


def factor_second_kernel(place, top, rest, out, out_half, w):
    w[...] = rest[128:, :]
    out[0] = top[...]

    def write(at, s):
        out[1, at:at + s.shape[0], :] = s[:, :128]
        out[2, at:at + s.shape[0], :] = s[:, 128:]

    eliminate(w, 128, 128, 256, write)
    out_half[...] = out[:, pl.ds(pl.multiple_of(place[0] * 64, 64), 64), :]


def fill_inverse(inv, place, around):
    core, x = place[0], place[1]
    inv[:, :128, 128:] = jnp.zeros((4, 128, 128), F32)

    def fill(k, blocks, at, size):
        for i, (row, col) in enumerate(((0, 0), (128, 0), (128, 128))):
            inv[k, pl.ds(pl.multiple_of(row + at, 64), size), col:col + 128] = blocks[i]

    own, near, other_near, far, other_far = around
    fill(x, own, 0, 128)
    fill((x + 2 * core - 1) & 3, near, 0, 128)
    fill((x - 2 * core + 1) & 3, other_near, 0, 128)
    fill((x + 2) & 3, far, core * 64, 64)
    fill((x + 2) & 3, other_far, (1 - core) * 64, 64)


def arrange_kernel(place, w0, w1, w2, w3, out):
    for j, pair in enumerate((w0, w1, w2, w3)):
        for a in range(2):
            out[a * 4 + (place[3] ^ (j >> 1)) * 2 + (place[4] ^ (j & 1))] = pair[a]


def right_kernel(place, w0, w1, w2, w3, l0, l1, l2, l3, l4, right_s, right_n, squares, inv):
    q = place[2]
    fill_inverse(inv, place, (l0, l1, l2, l3, l4))
    for j, w in enumerate((w0, w1, w2, w3)):
        p = q ^ j
        for k in range(2):
            rows = split(w[:, k * SQ:(k + 1) * SQ, :].reshape(8 * SQ, RANK))
            right_s[k, pl.ds(pl.multiple_of(p * 8 * SQ, 8 * SQ), 8 * SQ), :] = dot3(rows, split(inv[k]), NT)
        rows = split(w[:, 2 * SQ:, :].reshape(8 * NA, RANK))
        right_n[p >> 1, pl.ds(pl.multiple_of((p & 1) * 8 * NA, 8 * NA), 8 * NA), :] = dot3(
            rows, split(inv[2 + (p >> 1)]), NT
        )
    squares[...] = jnp.zeros_like(squares)
    for k in range(4):
        r = (right_s if k < 2 else right_n)[k % 2]
        squares[k:k + 1, :] = jnp.sum(r * r, axis=0, keepdims=True)


def momentum_kernel(place, l0, l1, l2, l3, l4, right_s, right_n, left, ms, gs, mn, gn, ortho, mom_s, mom_n, inv, s_out, n_out, sem):
    fill_inverse(inv, place, (l0, l1, l2, l3, l4))
    copies = []
    for k in range(4):
        m, g, right, mom, new = (ms, gs, right_s, mom_s, s_out) if k < 2 else (mn, gn, right_n, mom_n, n_out)
        o = dot3(split(left[k]), split(inv[k]), NT)
        ortho[k] = o
        low_rank = lax.dot_general(o.astype(BF16), right[k % 2].astype(BF16), NT, preferred_element_type=F32)
        new[k % 2] = (m[k % 2] + g[k % 2].astype(F32)) - (1.0 - 0.95) * low_rank
        copies.append(pltpu.make_async_copy(new.at[k % 2], mom.at[k % 2], sem.at[k]))
        copies[k].start()
    for copy in copies:
        copy.wait()


def update_kernel(place, q0, q1, q2, q3, right_s, right_n, ortho, up_s, basis_s, up_n, basis_n,
                  us_out, bs_out, un_out, bn_out, sem):
    scale = lax.rsqrt((q0[...] + q1[...]) + (q2[...] + q3[...]) + 1e-06)
    copies = []
    for k in range(4):
        right, up, basis, columns, u_out, b_out = (
            (right_s, up_s, basis_s, D, us_out, bs_out) if k < 2 else (right_n, up_n, basis_n, KVW, un_out, bn_out)
        )
        s = scale[k:k + 1, :]
        r = right[k % 2]
        b_out[k % 2] = r * s
        copies.append(pltpu.make_async_copy(b_out.at[k % 2], basis.at[k % 2], sem.at[0, k]))
        copies[-1].start()
        o = ortho[k] * (s * (D * columns / RANK) ** 0.5)
        u_out[k % 2] = dot3(split(o), split(r), NT).astype(BF16)
        copies.append(pltpu.make_async_copy(u_out.at[k % 2], up.at[k % 2], sem.at[1, k]))
        copies[-1].start()
    for copy in copies:
        copy.wait()


def partners():
    def pair(i, core, n):
        return ((i - core) % n ^ 1) + core

    def perm(move):
        at = [(i // 32, i // 8 % 4, i // 2 % 4, i % 2) for i in range(256)]
        out = []
        for i, (z, y, x, core) in enumerate(at):
            z, y = move(z, y, core)
            out.append((i, z % 8 * 32 + y % 4 * 8 + x * 2 + core))
        return out

    near_z = lambda z, core: pair(z, core, 8)
    near_y = lambda y, core: pair(y, core, 4)
    far_z = lambda z, core: pair(z // 2, core, 4) * 2 + z % 2
    near = [
        perm(lambda z, y, c: (z, near_y(y, c))),
        perm(lambda z, y, c: (near_z(z, c), y)),
        perm(lambda z, y, c: (near_z(z, c), near_y(y, c))),
    ]
    far = [
        perm(lambda z, y, c: (z, y + 2)),
        perm(lambda z, y, c: (far_z(z, c), y)),
        perm(lambda z, y, c: (far_z(z, c), y + 2)),
    ]
    sides = [(i, i // 8 * 8 + (i % 8 + (2 if i % 2 == 0 else 6)) % 8) for i in range(256)]
    return near, far, perm(lambda z, y, c: (z + 4, y)), sides


def shift_x(value, d):
    return lax.ppermute(value, "x", [(i, (i + d) % 4) for i in range(4)])


def around_x(value):
    got = {0: value}
    for d in (2, 1, 3):
        got[d] = shift_x(value, d)
    return [got[d] for d in range(4)]


def swap_core(value):
    return lax.ppermute(value, "core", [(0, 1), (1, 0)])


def local(mom_square, grad_square, basis_square, mom_narrow, grad_narrow, basis_narrow):
    zh, yh = lax.axis_index("zh"), lax.axis_index("yh")
    a, b = zh // 2, zh % 2
    q = lax.axis_index("zl") * 2 + lax.axis_index("yl")
    place = jnp.stack([lax.axis_index("core"), lax.axis_index("x"), q, b, yh]).astype(jnp.int32)
    near, far, across, sides = partners()
    send = lambda value, pairs: lax.ppermute(value, AXES, pairs)
    inputs = (mom_square, grad_square, basis_square, mom_narrow, grad_narrow, basis_narrow)

    buffers = (mom_square, grad_square, mom_narrow, grad_narrow)
    fetched = [pltpu.VMEM(v.shape, v.dtype) for v in buffers] + [pltpu.SemaphoreType.DMA((4,))]

    mine, theirs = call(
        project_kernel,
        [((4, 4, 32, RANK), F32)] * 2,
        (place,) + inputs,
        [pltpu.VMEM((4, 256, RANK), F32)]
        + [pltpu.VMEM(v.shape, v.dtype) for v in inputs]
        + [pltpu.SemaphoreType.DMA((6, 2))],
        name="project",
        far_in=range(1, 7),
    )
    half = mine + swap_core(theirs)
    chunks = [lax.dynamic_index_in_dim(half, (lax.axis_index("x") + d) % 4, 0, keepdims=False) for d in range(4)]
    chunks, buffers_late = lax.optimization_barrier((chunks, buffers))
    got = [shift_x(chunks[d], d) for d in (2, 1, 3)]
    transposes = call(
        prepare_kernel,
        [(v, BF16) for v in ((2, 1024, 256),) * 2 + ((2, 128, 256),) * 2],
        (place,) + buffers_late,
        fetched,
        name="prepare",
        far_in=range(1, 5),
    )
    got, transposes = lax.optimization_barrier((got, transposes))
    own_half = around_x((chunks[0] + got[0]) + (got[1] + got[2]))
    other_half = [swap_core(v) for v in own_half]

    left, own, *others = call(
        back_kernel,
        [((4, 256, RANK), F32)] + [((8 * CHUNK + 32, RANK), F32)] * 4,
        (place, *transposes, *own_half, *other_half),
        [pltpu.VMEM((32, CHUNK, RANK), F32), pltpu.VMEM((128, RANK), F32)],
        name="back",
    )
    got = [send(value, pairs) for value, pairs in zip(others[::-1], near[::-1])]
    mine, *others = call(meet_kernel, [((2 * CHUNK + 32, RANK), F32)] * 4, (place, own, *got), name="meet")
    got = [send(value, pairs) for value, pairs in zip(others[::-1], far[::-1])][::-1]
    own = mine + got[2] + got[1] + got[0]
    part = lambda i: jnp.concatenate([lax.dynamic_slice(own, (i * CHUNK, 0), (CHUNK, RANK)), own[2 * CHUNK:]])
    own = part(a) + send(part(1 - a), across)
    own, gram = own[:CHUNK], own[CHUNK:]
    got = send(own, across)
    (gram,) = stack(place, [gram] + [send(gram, pairs) for pairs in near])
    gram, got = lax.optimization_barrier((gram, got))
    other_gram = swap_core(gram)
    top, rest = call(
        factor_first_kernel,
        [((128, 128), F32), ((RANK, 2 * RANK), F32)],
        (place, gram, other_gram),
        name="factor_first",
    )
    pair = jnp.where(a == 0, jnp.stack([own, got]), jnp.stack([got, own]))
    pairs = [pair] + [send(pair, p) for p in far]
    top, rest, pairs = lax.optimization_barrier((top, rest, pairs))
    (quarter,) = call(arrange_kernel, [((8, CHUNK, RANK), F32)], (place, *pairs), name="arrange")
    quarters = [quarter] + [send(quarter, p) for p in near]
    blocks, half_blocks = call(
        factor_second_kernel,
        [((3, 128, 128), F32), ((3, 64, 128), F32)],
        (place, top, rest),
        [pltpu.VMEM((128, 2 * RANK), F32)],
        name="factor_second",
    )
    beside, apart = send(blocks, sides), shift_x(half_blocks, 2)
    around = blocks, beside, swap_core(beside), apart, swap_core(apart)
    inverse = pltpu.VMEM((4, RANK, RANK), F32)
    right_s, right_n, squares = call(
        right_kernel,
        [((2, 1024, RANK), F32), ((2, 128, RANK), F32), ((8, RANK), F32)],
        (place, *quarters, *around),
        [inverse],
        name="right",
    )
    squares, left = lax.optimization_barrier((squares + swap_core(squares), left))
    four_squares = around_x(squares)
    ortho, new_mom_s, new_mom_n = call(
        momentum_kernel,
        [((4, 256, RANK), F32), (mom_square.shape, F32), (mom_narrow.shape, F32)],
        (place, *around, right_s, right_n, left) + buffers,
        [inverse, pltpu.VMEM(mom_square.shape, F32), pltpu.VMEM(mom_narrow.shape, F32), pltpu.SemaphoreType.DMA((4,))],
        name="momentum",
        far_out=(1, 2),
    )
    outs = [(mom_square.shape, BF16), (basis_square.shape, F32), (mom_narrow.shape, BF16), (basis_narrow.shape, F32)]
    up_s, basis_s, up_n, basis_n = call(
        update_kernel,
        outs,
        (place, *four_squares, right_s, right_n, ortho),
        [pltpu.VMEM(*v) for v in outs] + [pltpu.SemaphoreType.DMA((2, 4))],
        name="update",
        far_out=range(4),
    )
    return new_mom_s, up_s, basis_s, new_mom_n, up_n, basis_n


def solution(mesh):
    fine = Mesh(mesh.devices.reshape(4, 2, 2, 2, 4, 2), AXES)
    matrix, factor = P(None, ROWS, COLS), P(None, COLS, None)
    return jax.shard_map(
        local,
        mesh=fine,
        in_specs=(matrix, matrix, factor) * 2,
        out_specs=(matrix, matrix, factor) * 2,
        check_vma=False,
    )
```
